32 devices in a mesh: coarse: 2 (over x), fine: 4 (over y, core), swath: 4 (over z).
Axes of the slice: x: 2, y: 2, z: 4, core: 2. Of those that a mesh axis runs over, the one named last changes fastest.
Arguments:
- echoes: int32 [32, 64, 2, 2048], P(('coarse', 'fine'), None, None, 'swath'), may hold values from -127 to 127
- exponents: int32 [32, 64, 64], P(('coarse', 'fine'), None, 'swath'), may hold values from 0 to 3
- replica: bfloat16 [2, 129], replicated, may hold values from -0.375 to 0.375
- interp0: bfloat16 [2, 32, 64, 64], P(None, ('coarse', 'fine')), may hold values from -0.5 to 0.5
- upsample1: bfloat16 [2, 32, 64, 512], P(None, ('coarse', 'fine')), may hold values from -0.1875 to 0.1875
- phase1: bfloat16 [512, 32, 2048], P(None, ('coarse', 'fine'), 'swath'), may hold values from -3.140625 to 3.140625
- upsample2: bfloat16 [4, 2, 512, 2048], P('coarse', None, 'fine'), may hold values from -0.09375 to 0.09375
- phase2: bfloat16 [2048, 4, 2048], P(None, 'coarse', 'swath'), may hold values from -3.140625 to 3.140625
Outputs:
- image: float32 [2048, 2, 2048], P(('coarse', 'fine'), None, 'swath')
The draws below stay inside these ranges and needn't reach their ends.
All inputs are finite; a program needn't handle non-finite values.
Results may differ from the reference program's by a relative error of at most 0.005.
Values may be sent and summed in bfloat16 or wider, within the bound.
A program may use at most 128 MiB of HBM per device.

```python
import jax
import jax.numpy as jnp
from jax import lax

HALF = 64
QB = 32
L = 64
GROUPS = 2
KIDS = 2
B0 = 64
B1 = 512
B2 = 2048
TAPS = 129
RANGE = 2048
SUBAPS = 32
PARENTS = 4
N_FINE = 4


def with_ends(values, rng, smallest, top_value):
    longest = values.shape.index(max(values.shape))
    spots = []
    for shift in (0, 1):
        where = [jax.random.randint(jax.random.fold_in(rng, axis), (), 0, length) for axis, length in enumerate(values.shape)]
        where[longest] = (where[longest] + shift) % values.shape[longest]
        spots.append(tuple(where))
    return values.at[spots[0]].set(smallest).at[spots[1]].set(top_value)


def steps_of(stream_key, dims, split, low, high):
    def one(dim, blocks):
        steps = jax.random.uniform(jax.random.fold_in(jax.random.fold_in(stream_key, 6), dim), (blocks,), jnp.float32, low / len(split), high / len(split))
        return jnp.repeat(jnp.exp(steps), dims[dim] // blocks).reshape((-1,) + (1,) * (len(dims) - dim - 1))

    loudness = one(*split[0])
    for cut in split[1:]:
        loudness = loudness * one(*cut)
    return loudness


def centred(own_key, dims, scale, limit, split=(), kind=jnp.bfloat16):
    values = scale * jax.random.normal(own_key, dims, jnp.float32)
    if split:
        values = values * steps_of(own_key, dims, split, -0.22, 0.18)
    return jnp.clip(values, -limit, limit).astype(kind)


def setup_inputs(seed: int = 0) -> dict:
    key_list = jax.random.split(jax.random.key(seed), 9)
    echoes = with_ends(jax.random.randint(key_list[0], (SUBAPS, L, 2, RANGE), -127, 128), jax.random.fold_in(key_list[0], 1), -127, 127).astype(jnp.int32)
    exponents = with_ends(jax.random.randint(key_list[1], (SUBAPS, L, RANGE // QB), 0, 4), jax.random.fold_in(key_list[1], 1), 0, 3).astype(jnp.int32)
    replica = centred(key_list[2], (2, TAPS), (2 * TAPS) ** -0.5, 0.375)
    interp0 = centred(key_list[3], (2, SUBAPS, L, B0), (2 * L) ** -0.5, 0.5, ((1, 8),))
    upsample1 = centred(key_list[4], (2, SUBAPS, B0, B1), (2 * B0 * KIDS * N_FINE) ** -0.5, 0.1875, ((1, 8),))
    phase1 = jnp.clip(jax.random.uniform(key_list[5], (B1, SUBAPS, RANGE), jnp.float32, -3.140625, 3.140625), -3.140625, 3.140625).astype(jnp.bfloat16)
    upsample2 = centred(key_list[6], (PARENTS, 2, B1, B2), (2 * B1 * PARENTS) ** -0.5, 0.09375, ((0, 2), (2, 4)))
    phase2 = jnp.clip(jax.random.uniform(key_list[7], (B2, PARENTS, RANGE), jnp.float32, -3.140625, 3.140625), -3.140625, 3.140625).astype(jnp.bfloat16)
    return {"echoes": echoes, "exponents": exponents, "replica": replica, "interp0": interp0, "upsample1": upsample1, "phase1": phase1, "upsample2": upsample2, "phase2": phase2}


def level_one(parent, echoes, exponents, kernel, interp0, upsample1, phase1):
    coarse_idx = parent // GROUPS
    group_idx = parent % GROUPS
    fine_ids = jnp.arange(N_FINE).astype(jnp.int32)
    kid_ids = jnp.arange(KIDS).astype(jnp.int32)
    members = ((coarse_idx * N_FINE + fine_ids[:, None]) * (GROUPS * KIDS) + group_idx * KIDS + kid_ids[None, :]).reshape(-1).astype(jnp.int32)
    quant = jnp.take(echoes, members, axis=0)
    expo = jnp.take(exponents, members, axis=0)
    factors = jnp.repeat(jnp.exp2(expo.astype(jnp.float32) - 8.0), QB, axis=2)
    samples = (quant.astype(jnp.float32) * factors[:, :, None, :]).astype(jnp.bfloat16)
    signal = samples.astype(jnp.float32).reshape(-1, 2, RANGE)
    compressed = lax.conv_general_dilated(signal, kernel, (1,), [(HALF, HALF)], precision=lax.Precision.HIGHEST)
    compressed = lax.optimization_barrier(compressed.astype(jnp.bfloat16)).astype(jnp.float32)
    compressed = compressed.reshape(-1, L, 2, RANGE)
    weight_table = jnp.take(interp0, members, axis=1).astype(jnp.float32)
    compressed_real = compressed[:, :, 0]
    compressed_imaginary = compressed[:, :, 1]
    beam_real_part = jnp.einsum("euj,eui->eji", weight_table[0], compressed_real) - jnp.einsum("euj,eui->eji", weight_table[1], compressed_imaginary)
    beam_imaginary_part = jnp.einsum("euj,eui->eji", weight_table[0], compressed_imaginary) + jnp.einsum("euj,eui->eji", weight_table[1], compressed_real)
    beam_real_part = lax.optimization_barrier(beam_real_part.astype(jnp.bfloat16)).astype(jnp.float32)
    beam_imaginary_part = lax.optimization_barrier(beam_imaginary_part.astype(jnp.bfloat16)).astype(jnp.float32)
    upper_bound = jnp.take(upsample1, members, axis=1).astype(jnp.float32)
    upsampled_real = jnp.einsum("xyj,xya->xja", upper_bound[0], beam_real_part) - jnp.einsum("xyj,xya->xja", upper_bound[1], beam_imaginary_part)
    upsampled_imaginary = jnp.einsum("xyj,xya->xja", upper_bound[0], beam_imaginary_part) + jnp.einsum("xyj,xya->xja", upper_bound[1], beam_real_part)
    angles = jnp.transpose(jnp.take(phase1, members, axis=1).astype(jnp.float32), (1, 0, 2))
    cosine = jnp.cos(angles)
    sine = jnp.sin(angles)
    level_re = jnp.sum(cosine * upsampled_real - sine * upsampled_imaginary, axis=0)
    level_im = jnp.sum(sine * upsampled_real + cosine * upsampled_imaginary, axis=0)
    level_re = lax.optimization_barrier(level_re.astype(jnp.bfloat16)).astype(jnp.float32)
    level_im = lax.optimization_barrier(level_im.astype(jnp.bfloat16)).astype(jnp.float32)
    return level_re, level_im


def reference(echoes, exponents, replica, interp0, upsample1, phase1, upsample2, phase2):
    tap_re = replica[0].astype(jnp.float32)
    tap_im = replica[1].astype(jnp.float32)
    kernel = jnp.stack([jnp.stack([tap_re, tap_im]), jnp.stack([-tap_im, tap_re])])

    def step(carry, parent):
        level_re, level_im = level_one(parent, echoes, exponents, kernel, interp0, upsample1, phase1)
        upper_bound = lax.dynamic_index_in_dim(upsample2, parent, 0, keepdims=False).astype(jnp.float32)
        val_re = jnp.dot(upper_bound[0].T, level_re, precision=lax.Precision.HIGHEST) - jnp.dot(upper_bound[1].T, level_im, precision=lax.Precision.HIGHEST)
        val_im = jnp.dot(upper_bound[0].T, level_im, precision=lax.Precision.HIGHEST) + jnp.dot(upper_bound[1].T, level_re, precision=lax.Precision.HIGHEST)
        angles = lax.dynamic_index_in_dim(phase2, parent, 1, keepdims=False).astype(jnp.float32)
        cosine = jnp.cos(angles)
        sine = jnp.sin(angles)
        term = jnp.stack([cosine * val_re - sine * val_im, sine * val_re + cosine * val_im], axis=1)
        return carry + term, None

    start_image = jnp.zeros((B2, 2, RANGE), jnp.float32)
    parents_all = jnp.arange(PARENTS).astype(jnp.int32)
    image, _ = lax.scan(step, start_image, parents_all)
    return image
```

```python
import functools

import jax
import jax.numpy as jnp
from jax import lax
from jax.experimental import pallas as pl
from jax.experimental.pallas import tpu as pltpu
from jax.sharding import PartitionSpec as P

MESH = pl.DeviceIdType.MESH
CHUNK = 128

SIN = (0.7071067690849304, -0.029462767764925957, 0.0003682722744997591, -2.1886112335778307e-06, 7.1958234926228215e-09)
COS = (1.4142135381698608, -0.17677636444568634, 0.0036825749557465315, -3.061256938963197e-05, 1.2790442838195304e-07)


def horner(coefs, u):
    total = coefs[-1] * u + coefs[-2]
    for coef in coefs[-3::-1]:
        total = total * u + coef
    return total


def cos_sin(angles):
    x = angles.astype(jnp.float32)
    u = x * x
    s = x * horner(SIN, u)
    c = horner(COS, u)
    return 1.0 - s * s, s * c


def mixed(values):
    re = values[:, :CHUNK]
    im = values[:, CHUNK:]
    return jnp.concatenate([values, jnp.concatenate([-im, re], axis=1)], axis=0)


def turned(values, angles):
    cosine, sine = cos_sin(angles)
    re = values[:, :CHUNK]
    im = values[:, CHUNK:]
    return cosine * re - sine * im, sine * re + cosine * im


def dot(a, b):
    return jnp.dot(a, b, preferred_element_type=jnp.float32)


def kernel(
    dims, samples, taps, w0, w1, ph1, u2, ph2, out,
    xs, halo_l, halo_r, band, rhs1, rhs2, u2m, pown, pms, pmr, ys, yr, lown, lmr, xsnd, xrcv, iown, y2s, y2r,
    u2_sem, halo_sem, core_sem, y_sem, l_sem, x_sem, y2_sem,
):
    C, Y, Z, G, K, S, L, B0, nb, wedge, NB, half = dims
    W = CHUNK
    R = NB * W
    c = lax.axis_index("coarse")
    f = lax.axis_index("fine")
    z = lax.axis_index("swath")
    y = f // 2
    k = f % 2
    mate = {"fine": y * 2 + 1 - k}

    def y_peer(d):
        return {"fine": ((y + d) % Y) * 2 + k}

    def x_peer(e):
        return {"coarse": (c + e) % C}

    barrier = pltpu.get_barrier_semaphore()
    partners = [mate] + [y_peer(d) for d in range(1, Y)] + [x_peer(e) for e in range(1, C)]
    for who in partners:
        pl.semaphore_signal(barrier, inc=1, device_id=who, device_id_type=MESH)

    @pl.when(z < Z - 1)
    def _():
        pl.semaphore_signal(barrier, inc=1, device_id={"swath": z + 1}, device_id_type=MESH)

    @pl.when(z > 0)
    def _():
        pl.semaphore_signal(barrier, inc=1, device_id={"swath": z - 1}, device_id_type=MESH)

    ends = jnp.where(z > 0, 1, 0) + jnp.where(z < Z - 1, 1, 0)
    pl.semaphore_wait(barrier, len(partners) + ends)

    def remote(src, dst, sems, who):
        return pltpu.make_async_remote_copy(
            src_ref=src, dst_ref=dst, send_sem=sems.at[0], recv_sem=sems.at[1], device_id=who, device_id_type=MESH
        )

    right = remote(samples.at[:, :, R - W : R], halo_l, halo_sem.at[0], {"swath": jnp.minimum(z + 1, Z - 1)})
    left = remote(samples.at[:, :, 0:W], halo_r, halo_sem.at[1], {"swath": jnp.maximum(z - 1, 0)})

    @pl.when(z < Z - 1)
    def _():
        right.start()

    @pl.when(z > 0)
    def _():
        left.start()

    u2_copy = remote(u2.at[1 - k], u2m, u2_sem, mate)
    u2_copy.start()
    sent = [u2_copy]

    reach = 3 * W
    width = taps.shape[1]
    toeplitz = []
    for part in range(2):
        row = jnp.broadcast_to(taps[part : part + 1, :], (reach, width))
        rolled = pltpu.roll(row, (half - W) % width, 1, stride=1, stride_axis=0)
        toeplitz.append(rolled[:, :W].astype(jnp.bfloat16))
    band[0, :, :W] = toeplitz[0]
    band[0, :, W:] = -toeplitz[1]
    band[1, :, :W] = toeplitz[1]
    band[1, :, W:] = toeplitz[0]
    xs[:, :, W : W + R] = samples[...]

    def fill_halo():
        @pl.when(z > 0)
        def _():
            right.wait_recv()
            xs[:, :, 0:W] = halo_l[...]

        @pl.when(z == 0)
        def _():
            xs[:, :, 0:W] = jnp.zeros((2, S * L, W), jnp.bfloat16)

        @pl.when(z < Z - 1)
        def _():
            left.wait_recv()
            xs[:, :, W + R : R + 2 * W] = halo_r[...]

        @pl.when(z == Z - 1)
        def _():
            xs[:, :, W + R : R + 2 * W] = jnp.zeros((2, S * L, W), jnp.bfloat16)

    core_copy, y_copy, l_copy, x_copy, y2_copy = {}, {}, {}, {}, {}
    sb1 = min(nb, 64)
    sb2 = min(wedge, 64)

    def level_one(j, nth):
        lanes = pl.ds(j * W, W)
        window = pl.ds(j * W, reach)
        comp = (dot(xs[0, :, window], band[0]) + dot(xs[1, :, window], band[1])).astype(jnp.bfloat16)
        for s in range(S):
            beams = dot(w0[s], mixed(comp[s * L : (s + 1) * L])).astype(jnp.bfloat16)
            rhs1[s] = mixed(beams)
        subs = nb // sb1

        def block(core, t):
            d = t // (G * subs)
            g = (t // subs) % G
            start = (t % subs) * sb1
            rows = pl.ds(pl.multiple_of((((y + d) % Y) * 2 + core) * nb + start, sb1), sb1)
            re = im = 0.0
            for kid in range(K):
                s = g * K + kid
                r, i = turned(dot(w1[s, rows, :], rhs1[s]), ph1[s, rows, lanes])
                re = re + r
                im = im + i
            return d, g, pl.ds(pl.multiple_of(start, sb1), sb1), re, im

        @pl.loop(0, Y * G * subs)
        def _(t):
            d, g, rows, re, im = block(1 - k, t)
            pms[nth, d, g, rows, :W] = re.astype(jnp.bfloat16)
            pms[nth, d, g, rows, W:] = im.astype(jnp.bfloat16)

        copy = remote(pms.at[nth], pmr.at[nth], core_sem.at[nth], mate)
        copy.start()
        core_copy[nth] = copy

        @pl.loop(0, Y * G * subs)
        def _(t):
            d, g, rows, re, im = block(k, t)
            pown[nth, d, g, rows, :W] = re
            pown[nth, d, g, rows, W:] = im

    def sum_cores(nth):
        core_copy[nth].wait_recv()
        for d in range(1, Y):
            for g in range(G):
                ys[nth, d - 1, g] = (pown[nth, d, g] + pmr[nth, d, g].astype(jnp.float32)).astype(jnp.bfloat16)
            copy = remote(ys.at[nth, d - 1], yr.at[nth, d - 1], y_sem.at[nth, d - 1], y_peer(d))
            copy.start()
            y_copy[nth, d] = copy

    def sum_y(nth):
        for d in range(1, Y):
            y_copy[nth, d].wait_recv()
        for g in range(G):
            total = pown[nth, 0, g] + pmr[nth, 0, g].astype(jnp.float32)
            for d in range(1, Y):
                total = total + yr[nth, d - 1, g].astype(jnp.float32)
            lown[nth, g] = total.astype(jnp.bfloat16)
        copy = remote(lown.at[nth], lmr.at[nth], l_sem.at[nth], mate)
        copy.start()
        l_copy[nth] = copy

    def level_two(j, nth):
        if nth == 0:
            u2_copy.wait_recv()
        l_copy[nth].wait_recv()
        lanes = pl.ds(j * W, W)
        for g in range(G):
            rhs2[g, 0] = mixed(lown[nth, g])
            rhs2[g, 1] = mixed(lmr[nth, g])
        subs = wedge // sb2

        def block(e, d, start):
            base = (((c + e) % C) * Y + (y + d) % Y) * wedge + start
            rows = pl.ds(pl.multiple_of(base, sb2), sb2)
            re = im = 0.0
            for g in range(G):
                values = dot(u2[k, g, rows, :], rhs2[g, 0]) + dot(u2m[g, rows, :], rhs2[g, 1])
                r, i = turned(values, ph2[g, rows, lanes])
                re = re + r
                im = im + i
            return re, im

        for e in range(1, C):

            @pl.loop(0, Y * subs)
            def _(t):
                d = t // subs
                start = (t % subs) * sb2
                rows = pl.ds(pl.multiple_of(start, sb2), sb2)
                re, im = block(e, d, start)
                xsnd[nth, e - 1, d, rows, :W] = re.astype(jnp.bfloat16)
                xsnd[nth, e - 1, d, rows, W:] = im.astype(jnp.bfloat16)

            copy = remote(xsnd.at[nth, e - 1], xrcv.at[nth, e - 1], x_sem.at[nth, e - 1], x_peer(e))
            copy.start()
            x_copy[nth, e] = copy

        @pl.loop(0, Y * subs)
        def _(t):
            d = t // subs
            start = (t % subs) * sb2
            rows = pl.ds(pl.multiple_of(start, sb2), sb2)
            re, im = block(0, d, start)
            iown[nth, d, rows, :W] = re
            iown[nth, d, rows, W:] = im

    def sum_x(nth):
        for e in range(1, C):
            x_copy[nth, e].wait_recv()
        for d in range(1, Y):
            total = iown[nth, d]
            for e in range(1, C):
                total = total + xrcv[nth, e - 1, d].astype(jnp.float32)
            y2s[nth, d - 1] = total.astype(jnp.bfloat16)
            copy = remote(y2s.at[nth, d - 1], y2r.at[nth, d - 1], y2_sem.at[nth, d - 1], y_peer(d))
            copy.start()
            y2_copy[nth, d] = copy

    def finish(j, nth):
        for d in range(1, Y):
            y2_copy[nth, d].wait_recv()
        total = iown[nth, 0]
        for e in range(1, C):
            total = total + xrcv[nth, e - 1, 0].astype(jnp.float32)
        for d in range(1, Y):
            total = total + y2r[nth, d - 1].astype(jnp.float32)
        out[:, j * W : (j + 1) * W] = total[:, :W]
        out[:, R + j * W : R + (j + 1) * W] = total[:, W:]

    order = list(range(1, NB - 1)) + [0, NB - 1]
    for t in range(NB + 5):
        if 0 <= t - 5 < NB:
            finish(order[t - 5], t - 5)
        if 0 <= t - 4 < NB:
            sum_x(t - 4)
        if 0 <= t - 2 < NB:
            sum_y(t - 2)
        if 0 <= t - 1 < NB:
            sum_cores(t - 1)
        if 0 <= t - 3 < NB:
            level_two(order[t - 3], t - 3)
        if t < NB:
            if order[t] == 0:
                fill_halo()
            level_one(order[t], t)

    for group in (core_copy, y_copy, l_copy, x_copy, y2_copy):
        sent.extend(group.values())
    for copy in sent:
        copy.wait_send()

    @pl.when(z < Z - 1)
    def _():
        right.wait_send()

    @pl.when(z > 0)
    def _():
        left.wait_send()


def shards(echoes, exponents, replica, interp0, upsample1, phase1, upsample2, phase2):
    S, L, _, R = echoes.shape
    G = upsample2.shape[0]
    B0 = interp0.shape[3]
    B1 = upsample1.shape[3]
    B2 = upsample2.shape[3]
    C, F, Z = lax.axis_size("coarse"), lax.axis_size("fine"), lax.axis_size("swath")
    Y = F // 2
    K = S // G
    nb = B1 // F
    wedge = B2 // (C * F)
    W = CHUNK
    NB = R // W
    taps_count = replica.shape[1]
    half = (taps_count - 1) // 2
    bf16, f32 = jnp.bfloat16, jnp.float32

    factors = jnp.repeat(jnp.exp2(exponents.astype(f32) - 8.0), R // exponents.shape[2], axis=2)
    samples = (echoes.astype(f32) * factors[:, :, None, :]).astype(bf16)
    samples = samples.transpose(2, 0, 1, 3).reshape(2, S * L, R)
    width = 4 * W
    line = replica.astype(f32)
    taps = jnp.concatenate([line[:, :1], jnp.zeros((2, width - taps_count), f32), line[:, :0:-1]], axis=1)
    w0 = interp0.transpose(1, 3, 0, 2).reshape(S, B0, 2 * L)
    w1 = upsample1.transpose(1, 3, 0, 2).reshape(S, B1, 2 * B0)
    ph1 = phase1.transpose(1, 0, 2)
    u2 = upsample2.reshape(G, 2, nb, C * Y, 2, wedge).transpose(4, 0, 3, 5, 1, 2).reshape(2, G, C * Y * wedge, 2 * nb)
    core = lax.axis_index("fine") % 2
    ph2 = lax.dynamic_index_in_dim(phase2.reshape(C * Y, 2, wedge, G, R), core, 1, keepdims=False)
    ph2 = ph2.reshape(C * Y * wedge, G, R).transpose(1, 0, 2)

    dims = (C, Y, Z, G, K, S, L, B0, nb, wedge, NB, half)
    dma = pltpu.SemaphoreType.DMA
    vm = pltpu.VMEM
    spec = pl.BlockSpec(memory_space=pltpu.VMEM)
    flat = pl.pallas_call(
        functools.partial(kernel, dims),
        out_shape=jax.ShapeDtypeStruct((wedge, 2 * R), f32),
        in_specs=[spec] * 7,
        out_specs=spec,
        scratch_shapes=[
            vm((2, S * L, R + 2 * W), bf16),
            vm((2, S * L, W), bf16),
            vm((2, S * L, W), bf16),
            vm((2, 3 * W, 2 * W), bf16),
            vm((S, 2 * B0, 2 * W), bf16),
            vm((G, 2, 2 * nb, 2 * W), bf16),
            vm((G, C * Y * wedge, 2 * nb), bf16),
            vm((NB, Y, G, nb, 2 * W), f32),
            vm((NB, Y, G, nb, 2 * W), bf16),
            vm((NB, Y, G, nb, 2 * W), bf16),
            vm((NB, Y - 1, G, nb, 2 * W), bf16),
            vm((NB, Y - 1, G, nb, 2 * W), bf16),
            vm((NB, G, nb, 2 * W), bf16),
            vm((NB, G, nb, 2 * W), bf16),
            vm((NB, C - 1, Y, wedge, 2 * W), bf16),
            vm((NB, C - 1, Y, wedge, 2 * W), bf16),
            vm((NB, Y, wedge, 2 * W), f32),
            vm((NB, Y - 1, wedge, 2 * W), bf16),
            vm((NB, Y - 1, wedge, 2 * W), bf16),
            dma((2,)),
            dma((2, 2)),
            dma((NB, 2)),
            dma((NB, Y - 1, 2)),
            dma((NB, 2)),
            dma((NB, C - 1, 2)),
            dma((NB, Y - 1, 2)),
        ],
        compiler_params=pltpu.CompilerParams(
            collective_id=0, has_side_effects=True, vmem_limit_bytes=48 * 1024 * 1024
        ),
    )(samples, taps, w0, w1, ph1, u2, ph2)
    return flat.reshape(wedge, 2, R)


def solution(mesh):
    in_specs = (
        P(("coarse", "fine"), None, None, "swath"),
        P(("coarse", "fine"), None, "swath"),
        P(),
        P(None, ("coarse", "fine"), None, None),
        P(None, ("coarse", "fine"), None, None),
        P(None, ("coarse", "fine"), "swath"),
        P("coarse", None, "fine", None),
        P(None, "coarse", "swath"),
    )
    out_specs = P(("coarse", "fine"), None, "swath")
    return jax.shard_map(shards, mesh=mesh, in_specs=in_specs, out_specs=out_specs, check_vma=False)
```

```python
import functools

import jax
import jax.numpy as jnp
from jax import lax
from jax.experimental import pallas as pl
from jax.experimental.pallas import tpu as pltpu
from jax.sharding import PartitionSpec as P

MESH = pl.DeviceIdType.MESH
CHUNK = 128

SIN = (0.7071067690849304, -0.029462767764925957, 0.0003682722744997591, -2.1886112335778307e-06, 7.1958234926228215e-09)
COS = (1.4142135381698608, -0.17677636444568634, 0.0036825749557465315, -3.061256938963197e-05, 1.2790442838195304e-07)


def horner(coefs, u):
    total = coefs[-1] * u + coefs[-2]
    for coef in coefs[-3::-1]:
        total = total * u + coef
    return total


def cos_sin(angles):
    x = angles.astype(jnp.float32)
    u = x * x
    s = x * horner(SIN, u)
    c = horner(COS, u)
    return 1.0 - s * s, s * c


def mixed(values):
    re = values[:, :CHUNK]
    im = values[:, CHUNK:]
    return jnp.concatenate([values, jnp.concatenate([-im, re], axis=1)], axis=0)


def turned(values, angles):
    cosine, sine = cos_sin(angles)
    re = values[:, :CHUNK]
    im = values[:, CHUNK:]
    return cosine * re - sine * im, sine * re + cosine * im


def dot(a, b):
    return jnp.dot(a, b, preferred_element_type=jnp.float32)


def kernel(
    dims, samples, taps, interp0, upsample1, ph1, u2, ph2, out,
    w0, w1, u2t, xs, halo_l, halo_r, band, rhs1, rhs2, u2m, pown, pms, pmr, ys, yr, lown, lmr, xsnd, xrcv, iown, y2s, y2r,
    u2_sem, halo_sem, core_sem, y_sem, l_sem, x_sem, y2_sem,
):
    C, Y, Z, G, K, S, L, B0, nb, wedge, NB, half = dims
    W = CHUNK
    R = NB * W
    c = lax.axis_index("coarse")
    f = lax.axis_index("fine")
    z = lax.axis_index("swath")
    y = f // 2
    k = f % 2
    mate = {"fine": y * 2 + 1 - k}

    def y_peer(d):
        return {"fine": ((y + d) % Y) * 2 + k}

    def x_peer(e):
        return {"coarse": (c + e) % C}

    barrier = pltpu.get_barrier_semaphore()
    partners = [mate] + [y_peer(d) for d in range(1, Y)] + [x_peer(e) for e in range(1, C)]
    for who in partners:
        pl.semaphore_signal(barrier, inc=1, device_id=who, device_id_type=MESH)

    @pl.when(z < Z - 1)
    def _():
        pl.semaphore_signal(barrier, inc=1, device_id={"swath": z + 1}, device_id_type=MESH)

    @pl.when(z > 0)
    def _():
        pl.semaphore_signal(barrier, inc=1, device_id={"swath": z - 1}, device_id_type=MESH)

    ends = jnp.where(z > 0, 1, 0) + jnp.where(z < Z - 1, 1, 0)
    pl.semaphore_wait(barrier, len(partners) + ends)

    def remote(src, dst, sems, who):
        return pltpu.make_async_remote_copy(
            src_ref=src, dst_ref=dst, send_sem=sems.at[0], recv_sem=sems.at[1], device_id=who, device_id_type=MESH
        )

    right = remote(samples.at[:, :, R - W : R], halo_l, halo_sem.at[0], {"swath": jnp.minimum(z + 1, Z - 1)})
    left = remote(samples.at[:, :, 0:W], halo_r, halo_sem.at[1], {"swath": jnp.maximum(z - 1, 0)})

    @pl.when(z < Z - 1)
    def _():
        right.start()

    @pl.when(z > 0)
    def _():
        left.start()

    for s in range(S):
        w0[s] = jnp.concatenate([interp0[0, s], interp0[1, s]], axis=0).T
        w1[s] = jnp.concatenate([upsample1[0, s], upsample1[1, s]], axis=0).T

    reach = 3 * W
    width = taps.shape[1]
    toeplitz = []
    for part in range(2):
        row = jnp.broadcast_to(taps[part : part + 1, :], (reach, width))
        rolled = pltpu.roll(row, (half - W) % width, 1, stride=1, stride_axis=0)
        toeplitz.append(rolled[:, :W].astype(jnp.bfloat16))
    band[0, :, :W] = toeplitz[0]
    band[0, :, W:] = -toeplitz[1]
    band[1, :, :W] = toeplitz[1]
    band[1, :, W:] = toeplitz[0]
    xs[:, :, W : W + R] = samples[...]

    def fill_halo():
        @pl.when(z > 0)
        def _():
            right.wait_recv()
            xs[:, :, 0:W] = halo_l[...]

        @pl.when(z == 0)
        def _():
            xs[:, :, 0:W] = jnp.zeros((2, S * L, W), jnp.bfloat16)

        @pl.when(z < Z - 1)
        def _():
            left.wait_recv()
            xs[:, :, W + R : R + 2 * W] = halo_r[...]

        @pl.when(z == Z - 1)
        def _():
            xs[:, :, W + R : R + 2 * W] = jnp.zeros((2, S * L, W), jnp.bfloat16)

    core_copy, y_copy, l_copy, x_copy, y2_copy = {}, {}, {}, {}, {}
    u2_copy = remote(u2t.at[:, :, 1 - k], u2m, u2_sem, mate)
    sub = 64

    def turn_columns():
        step = max(wedge, W)
        for g in range(G):
            for first in range(0, u2.shape[3], step):
                block = u2[g, :, :, first : first + step].reshape(2 * nb, step).T
                for i in range(step // wedge):
                    q = first // wedge + i
                    u2t[g, q // 2, q % 2] = block[i * wedge : (i + 1) * wedge]
        u2_copy.start()

    def level_one(j, nth):
        lanes = pl.ds(j * W, W)
        window = pl.ds(j * W, reach)
        comp = (dot(xs[0, :, window], band[0]) + dot(xs[1, :, window], band[1])).astype(jnp.bfloat16)
        for s in range(S):
            beams = dot(w0[s], mixed(comp[s * L : (s + 1) * L])).astype(jnp.bfloat16)
            rhs1[s] = mixed(beams)
        def block(core, d, store):
            base = pl.multiple_of((((y + d) % Y) * 2 + core) * nb, nb)
            for g in range(G):
                values = [dot(w1[g * K + kid, pl.ds(base, nb), :], rhs1[g * K + kid]) for kid in range(K)]
                for start in range(0, nb, sub):
                    size = min(sub, nb - start)
                    rows = pl.ds(pl.multiple_of(base + start, size), size)
                    re = im = 0.0
                    for kid in range(K):
                        r, i = turned(values[kid][start : start + size], ph1[g * K + kid, rows, lanes])
                        re = re + r
                        im = im + i
                    store[g, start : start + size, :W] = re.astype(store.dtype)
                    store[g, start : start + size, W:] = im.astype(store.dtype)

        offsets = list(range(1, Y)) + [0]
        for d in offsets:
            block(1 - k, d, pms.at[nth, d])
            copy = remote(pms.at[nth, d], pmr.at[nth, d], core_sem.at[nth, d], mate)
            copy.start()
            core_copy[nth, d] = copy
        for d in offsets:
            block(k, d, pown.at[nth, d])

    def sum_cores(nth):
        for d in range(1, Y):
            core_copy[nth, d].wait_recv()
            for g in range(G):
                ys[nth, d - 1, g] = (pown[nth, d, g] + pmr[nth, d, g].astype(jnp.float32)).astype(jnp.bfloat16)
            copy = remote(ys.at[nth, d - 1], yr.at[nth, d - 1], y_sem.at[nth, d - 1], y_peer(d))
            copy.start()
            y_copy[nth, d] = copy

    def sum_y(nth):
        core_copy[nth, 0].wait_recv()
        for d in range(1, Y):
            y_copy[nth, d].wait_recv()
        for g in range(G):
            total = pown[nth, 0, g] + pmr[nth, 0, g].astype(jnp.float32)
            for d in range(1, Y):
                total = total + yr[nth, d - 1, g].astype(jnp.float32)
            lown[nth, g] = total.astype(jnp.bfloat16)
        copy = remote(lown.at[nth], lmr.at[nth], l_sem.at[nth], mate)
        copy.start()
        l_copy[nth] = copy

    def level_two(j, nth):
        if nth == 0:
            u2_copy.wait_recv()
        l_copy[nth].wait_recv()
        lanes = pl.ds(j * W, W)
        for g in range(G):
            rhs2[g, : 2 * nb] = mixed(lown[nth, g])
            rhs2[g, 2 * nb :] = mixed(lmr[nth, g])

        def block(e, d, store):
            q = ((c + e) % C) * Y + (y + d) % Y
            values = [dot(jnp.concatenate([u2t[g, q, k], u2m[g, q]], axis=1), rhs2[g]) for g in range(G)]
            for start in range(0, wedge, sub):
                size = min(sub, wedge - start)
                re = im = 0.0
                for g in range(G):
                    r, i = turned(values[g][start : start + size], ph2[g, q, k, start : start + size, lanes])
                    re = re + r
                    im = im + i
                store[start : start + size, :W] = re.astype(store.dtype)
                store[start : start + size, W:] = im.astype(store.dtype)

        offsets = list(range(1, Y)) + [0]
        for e in range(1, C):
            for d in offsets:
                block(e, d, xsnd.at[nth, e - 1, d])
                copy = remote(xsnd.at[nth, e - 1, d], xrcv.at[nth, e - 1, d], x_sem.at[nth, e - 1, d], x_peer(e))
                copy.start()
                x_copy[nth, e, d] = copy
        for d in offsets:
            block(0, d, iown.at[nth, d])

    def sum_x(nth):
        for d in range(1, Y):
            total = iown[nth, d]
            for e in range(1, C):
                x_copy[nth, e, d].wait_recv()
                total = total + xrcv[nth, e - 1, d].astype(jnp.float32)
            y2s[nth, d - 1] = total.astype(jnp.bfloat16)
            copy = remote(y2s.at[nth, d - 1], y2r.at[nth, d - 1], y2_sem.at[nth, d - 1], y_peer(d))
            copy.start()
            y2_copy[nth, d] = copy

    def finish(j, nth):
        for d in range(1, Y):
            y2_copy[nth, d].wait_recv()
        total = iown[nth, 0]
        for e in range(1, C):
            x_copy[nth, e, 0].wait_recv()
            total = total + xrcv[nth, e - 1, 0].astype(jnp.float32)
        for d in range(1, Y):
            total = total + y2r[nth, d - 1].astype(jnp.float32)
        out[:, j * W : (j + 1) * W] = total[:, :W]
        out[:, R + j * W : R + (j + 1) * W] = total[:, W:]

    order = list(range(1, NB - 1)) + [0, NB - 1]
    for t in range(NB + 5):
        if t < NB:
            if order[t] == 0:
                fill_halo()
            level_one(order[t], t)
        if t == 0:
            turn_columns()
        if 0 <= t - 2 < NB:
            level_two(order[t - 2], t - 2)
        if t < NB:
            sum_cores(t)
        if 0 <= t - 1 < NB:
            sum_y(t - 1)
        if 0 <= t - 4 < NB:
            sum_x(t - 4)
        if 0 <= t - 5 < NB:
            finish(order[t - 5], t - 5)

    sent = [u2_copy]
    for group in (core_copy, y_copy, l_copy, x_copy, y2_copy):
        sent.extend(group.values())
    for copy in sent:
        copy.wait_send()

    @pl.when(z < Z - 1)
    def _():
        right.wait_send()

    @pl.when(z > 0)
    def _():
        left.wait_send()


def shards(echoes, exponents, replica, interp0, upsample1, phase1, upsample2, phase2):
    S, L, _, R = echoes.shape
    G = upsample2.shape[0]
    B0 = interp0.shape[3]
    B1 = upsample1.shape[3]
    B2 = upsample2.shape[3]
    C, F, Z = lax.axis_size("coarse"), lax.axis_size("fine"), lax.axis_size("swath")
    Y = F // 2
    K = S // G
    nb = B1 // F
    wedge = B2 // (C * F)
    W = CHUNK
    NB = R // W
    taps_count = replica.shape[1]
    half = (taps_count - 1) // 2
    bf16, f32 = jnp.bfloat16, jnp.float32

    factors = jnp.repeat(jnp.exp2(exponents.astype(f32) - 8.0), R // exponents.shape[2], axis=2)
    samples = (echoes.astype(f32) * factors[:, :, None, :]).astype(bf16)
    samples = samples.transpose(2, 0, 1, 3).reshape(2, S * L, R)
    width = 4 * W
    line = replica.astype(f32)
    taps = jnp.concatenate([line[:, :1], jnp.zeros((2, width - taps_count), f32), line[:, :0:-1]], axis=1)
    ph1 = phase1.transpose(1, 0, 2)
    ph2 = phase2.transpose(1, 0, 2).reshape(G, C * Y, 2, wedge, R)

    dims = (C, Y, Z, G, K, S, L, B0, nb, wedge, NB, half)
    dma = pltpu.SemaphoreType.DMA
    vm = pltpu.VMEM
    spec = pl.BlockSpec(memory_space=pltpu.VMEM)
    flat = pl.pallas_call(
        functools.partial(kernel, dims),
        out_shape=jax.ShapeDtypeStruct((wedge, 2 * R), f32),
        in_specs=[spec] * 7,
        out_specs=spec,
        scratch_shapes=[
            vm((S, B0, 2 * L), bf16),
            vm((S, B1, 2 * B0), bf16),
            vm((G, C * Y, 2, wedge, 2 * nb), bf16),
            vm((2, S * L, R + 2 * W), bf16),
            vm((2, S * L, W), bf16),
            vm((2, S * L, W), bf16),
            vm((2, 3 * W, 2 * W), bf16),
            vm((S, 2 * B0, 2 * W), bf16),
            vm((G, 4 * nb, 2 * W), bf16),
            vm((G, C * Y, wedge, 2 * nb), bf16),
            vm((NB, Y, G, nb, 2 * W), f32),
            vm((NB, Y, G, nb, 2 * W), bf16),
            vm((NB, Y, G, nb, 2 * W), bf16),
            vm((NB, Y - 1, G, nb, 2 * W), bf16),
            vm((NB, Y - 1, G, nb, 2 * W), bf16),
            vm((NB, G, nb, 2 * W), bf16),
            vm((NB, G, nb, 2 * W), bf16),
            vm((NB, C - 1, Y, wedge, 2 * W), bf16),
            vm((NB, C - 1, Y, wedge, 2 * W), bf16),
            vm((NB, Y, wedge, 2 * W), f32),
            vm((NB, Y - 1, wedge, 2 * W), bf16),
            vm((NB, Y - 1, wedge, 2 * W), bf16),
            dma((2,)),
            dma((2, 2)),
            dma((NB, Y, 2)),
            dma((NB, Y - 1, 2)),
            dma((NB, 2)),
            dma((NB, C - 1, Y, 2)),
            dma((NB, Y - 1, 2)),
        ],
        compiler_params=pltpu.CompilerParams(
            collective_id=0, has_side_effects=True, vmem_limit_bytes=28 * 1024 * 1024
        ),
    )(samples, taps, interp0, upsample1, ph1, upsample2, ph2)
    return flat.reshape(wedge, 2, R)


def solution(mesh):
    in_specs = (
        P(("coarse", "fine"), None, None, "swath"),
        P(("coarse", "fine"), None, "swath"),
        P(),
        P(None, ("coarse", "fine"), None, None),
        P(None, ("coarse", "fine"), None, None),
        P(None, ("coarse", "fine"), "swath"),
        P("coarse", None, "fine", None),
        P(None, "coarse", "swath"),
    )
    out_specs = P(("coarse", "fine"), None, "swath")
    return jax.shard_map(shards, mesh=mesh, in_specs=in_specs, out_specs=out_specs, check_vma=False)
```

```python
import functools

import jax
import jax.numpy as jnp
from jax import lax
from jax.experimental import pallas as pl
from jax.experimental.pallas import tpu as pltpu
from jax.sharding import PartitionSpec as P

MESH = pl.DeviceIdType.MESH
CHUNK = 128

SIN = (0.7071067690849304, -0.029462767764925957, 0.0003682722744997591, -2.1886112335778307e-06, 7.1958234926228215e-09)
COS = (1.4142135381698608, -0.17677636444568634, 0.0036825749557465315, -3.061256938963197e-05, 1.2790442838195304e-07)


def horner(coefs, u):
    total = coefs[-1] * u + coefs[-2]
    for coef in coefs[-3::-1]:
        total = total * u + coef
    return total


def cos_sin(angles):
    x = angles.astype(jnp.float32)
    u = x * x
    s = x * horner(SIN, u)
    c = horner(COS, u)
    return 1.0 - s * s, s * c


def mixed(values):
    re = values[:, :CHUNK]
    im = values[:, CHUNK:]
    return jnp.concatenate([values, jnp.concatenate([-im, re], axis=1)], axis=0)


def turned(values, angles):
    cosine, sine = cos_sin(angles)
    re = values[:, :CHUNK]
    im = values[:, CHUNK:]
    return cosine * re - sine * im, sine * re + cosine * im


def dot(a, b):
    return jnp.dot(a, b, preferred_element_type=jnp.float32)


def kernel(
    dims, echoes, exponents, replica, interp0, upsample1, ph1, u2_hbm, ph2, out,
    hp, u2, w0, w1, u2t, xs, halo_l, halo_r, band, rhs1, rhs2, u2m, pown, pms, pmr, ys, yr, lown, lmr, xsnd, xrcv, iown, y2s, y2r,
    load_sem, u2_sem, halo_sem, core_sem, y_sem, l_sem, x_sem, y2_sem,
):
    C, Y, Z, G, K, S, L, B0, nb, wedge, NB, half = dims
    W = CHUNK
    R = NB * W
    c = lax.axis_index("coarse")
    f = lax.axis_index("fine")
    z = lax.axis_index("swath")
    y = f // 2
    k = f % 2
    mate = {"fine": y * 2 + 1 - k}

    def y_peer(d):
        return {"fine": ((y + d) % Y) * 2 + k}

    def x_peer(e):
        return {"coarse": (c + e) % C}

    load = pltpu.make_async_copy(u2_hbm, u2, load_sem.at[0])
    load.start()

    barrier = pltpu.get_barrier_semaphore()
    partners = [mate] + [y_peer(d) for d in range(1, Y)] + [x_peer(e) for e in range(1, C)]
    for who in partners:
        pl.semaphore_signal(barrier, inc=1, device_id=who, device_id_type=MESH)

    @pl.when(z < Z - 1)
    def _():
        pl.semaphore_signal(barrier, inc=1, device_id={"swath": z + 1}, device_id_type=MESH)

    @pl.when(z > 0)
    def _():
        pl.semaphore_signal(barrier, inc=1, device_id={"swath": z - 1}, device_id_type=MESH)

    blocks = exponents.shape[1]
    spread = lax.broadcasted_iota(jnp.int32, (blocks, R), 1) // (R // blocks)
    spread = (spread == lax.broadcasted_iota(jnp.int32, (blocks, R), 0)).astype(jnp.bfloat16)
    for s in range(S):
        powers = jnp.left_shift(jnp.ones_like(exponents[s]), exponents[s]).astype(jnp.float32) * 2.0**-8
        factors = dot(powers.T.astype(jnp.bfloat16), spread)
        for part in range(2):
            values = echoes[s, :, part, :].astype(jnp.float32) * factors
            xs[part, s * L : (s + 1) * L, W : W + R] = values.astype(jnp.bfloat16)

    ends = jnp.where(z > 0, 1, 0) + jnp.where(z < Z - 1, 1, 0)
    pl.semaphore_wait(barrier, len(partners) + ends)

    def remote(src, dst, sems, who):
        return pltpu.make_async_remote_copy(
            src_ref=src, dst_ref=dst, send_sem=sems.at[0], recv_sem=sems.at[1], device_id=who, device_id_type=MESH
        )

    right = remote(xs.at[:, :, pl.ds(R, W)], halo_l, halo_sem.at[0], {"swath": jnp.minimum(z + 1, Z - 1)})
    left = remote(xs.at[:, :, pl.ds(W, W)], halo_r, halo_sem.at[1], {"swath": jnp.maximum(z - 1, 0)})

    @pl.when(z < Z - 1)
    def _():
        right.start()

    @pl.when(z > 0)
    def _():
        left.start()

    for s in range(S):
        w0[s] = jnp.concatenate([interp0[0, s], interp0[1, s]], axis=0).T
        w1[s] = jnp.concatenate([upsample1[0, s], upsample1[1, s]], axis=0).T

    reach = 3 * W
    hp[...] = jnp.zeros_like(hp)
    hp[:, : replica.shape[1]] = replica[...].astype(jnp.float32)
    toeplitz = []
    for part in range(2):
        row = jnp.broadcast_to(hp[part : part + 1, :], (W, reach))
        rolled = pltpu.roll(row, W - half, 1, stride=1, stride_axis=0)
        toeplitz.append(rolled.T.astype(jnp.bfloat16))
    band[0, :, :W] = toeplitz[0]
    band[0, :, W:] = -toeplitz[1]
    band[1, :, :W] = toeplitz[1]
    band[1, :, W:] = toeplitz[0]

    def fill_halo():
        @pl.when(z > 0)
        def _():
            right.wait_recv()
            xs[:, :, 0:W] = halo_l[...]

        @pl.when(z == 0)
        def _():
            xs[:, :, 0:W] = jnp.zeros((2, S * L, W), jnp.bfloat16)

        @pl.when(z < Z - 1)
        def _():
            left.wait_recv()
            xs[:, :, W + R : R + 2 * W] = halo_r[...]

        @pl.when(z == Z - 1)
        def _():
            xs[:, :, W + R : R + 2 * W] = jnp.zeros((2, S * L, W), jnp.bfloat16)

    core_copy, y_copy, l_copy, x_copy, y2_copy = {}, {}, {}, {}, {}
    u2_copy = remote(u2t.at[:, :, 1 - k], u2m, u2_sem, mate)
    sub = 64

    def turn_columns():
        load.wait()
        step = max(wedge, W)
        for g in range(G):
            for first in range(0, u2.shape[3], step):
                block = u2[g, :, :, first : first + step].reshape(2 * nb, step).T
                for i in range(step // wedge):
                    q = first // wedge + i
                    u2t[g, q // 2, q % 2] = block[i * wedge : (i + 1) * wedge]
        u2_copy.start()

    def level_one(j, nth):
        lanes = pl.ds(j * W, W)
        window = pl.ds(j * W, reach)
        comp = (dot(xs[0, :, window], band[0]) + dot(xs[1, :, window], band[1])).astype(jnp.bfloat16)
        for s in range(S):
            beams = dot(w0[s], mixed(comp[s * L : (s + 1) * L])).astype(jnp.bfloat16)
            rhs1[s] = mixed(beams)
        def block(core, d, store):
            base = pl.multiple_of((((y + d) % Y) * 2 + core) * nb, nb)
            for g in range(G):
                values = [dot(w1[g * K + kid, pl.ds(base, nb), :], rhs1[g * K + kid]) for kid in range(K)]
                for start in range(0, nb, sub):
                    size = min(sub, nb - start)
                    rows = pl.ds(pl.multiple_of(base + start, size), size)
                    re = im = 0.0
                    for kid in range(K):
                        r, i = turned(values[kid][start : start + size], ph1[g * K + kid, rows, lanes])
                        re = re + r
                        im = im + i
                    store[g, start : start + size, :W] = re.astype(store.dtype)
                    store[g, start : start + size, W:] = im.astype(store.dtype)

        offsets = list(range(1, Y)) + [0]
        for d in offsets:
            block(1 - k, d, pms.at[nth, d])
            copy = remote(pms.at[nth, d], pmr.at[nth, d], core_sem.at[nth, d], mate)
            copy.start()
            core_copy[nth, d] = copy
        for d in offsets:
            block(k, d, pown.at[nth, d])

    def sum_cores(nth):
        for d in range(1, Y):
            core_copy[nth, d].wait_recv()
            for g in range(G):
                ys[nth, d - 1, g] = (pown[nth, d, g] + pmr[nth, d, g].astype(jnp.float32)).astype(jnp.bfloat16)
            copy = remote(ys.at[nth, d - 1], yr.at[nth, d - 1], y_sem.at[nth, d - 1], y_peer(d))
            copy.start()
            y_copy[nth, d] = copy

    def sum_y(nth):
        core_copy[nth, 0].wait_recv()
        for d in range(1, Y):
            y_copy[nth, d].wait_recv()
        for g in range(G):
            total = pown[nth, 0, g] + pmr[nth, 0, g].astype(jnp.float32)
            for d in range(1, Y):
                total = total + yr[nth, d - 1, g].astype(jnp.float32)
            lown[nth, g] = total.astype(jnp.bfloat16)
        copy = remote(lown.at[nth], lmr.at[nth], l_sem.at[nth], mate)
        copy.start()
        l_copy[nth] = copy

    def level_two(j, nth):
        if nth == 0:
            u2_copy.wait_recv()
        l_copy[nth].wait_recv()
        lanes = pl.ds(j * W, W)
        for g in range(G):
            rhs2[g, : 2 * nb] = mixed(lown[nth, g])
            rhs2[g, 2 * nb :] = mixed(lmr[nth, g])

        def block(e, d, store):
            q = ((c + e) % C) * Y + (y + d) % Y
            values = [dot(jnp.concatenate([u2t[g, q, k], u2m[g, q]], axis=1), rhs2[g]) for g in range(G)]
            for start in range(0, wedge, sub):
                size = min(sub, wedge - start)
                re = im = 0.0
                for g in range(G):
                    r, i = turned(values[g][start : start + size], ph2[g, q, k, start : start + size, lanes])
                    re = re + r
                    im = im + i
                store[start : start + size, :W] = re.astype(store.dtype)
                store[start : start + size, W:] = im.astype(store.dtype)

        offsets = list(range(1, Y)) + [0]
        for e in range(1, C):
            for d in offsets:
                block(e, d, xsnd.at[nth, e - 1, d])
                copy = remote(xsnd.at[nth, e - 1, d], xrcv.at[nth, e - 1, d], x_sem.at[nth, e - 1, d], x_peer(e))
                copy.start()
                x_copy[nth, e, d] = copy
        for d in offsets:
            block(0, d, iown.at[nth, d])

    def sum_x(nth):
        for d in range(1, Y):
            total = iown[nth, d]
            for e in range(1, C):
                x_copy[nth, e, d].wait_recv()
                total = total + xrcv[nth, e - 1, d].astype(jnp.float32)
            y2s[nth, d - 1] = total.astype(jnp.bfloat16)
            copy = remote(y2s.at[nth, d - 1], y2r.at[nth, d - 1], y2_sem.at[nth, d - 1], y_peer(d))
            copy.start()
            y2_copy[nth, d] = copy

    def finish(j, nth):
        for d in range(1, Y):
            y2_copy[nth, d].wait_recv()
        total = iown[nth, 0]
        for e in range(1, C):
            x_copy[nth, e, 0].wait_recv()
            total = total + xrcv[nth, e - 1, 0].astype(jnp.float32)
        for d in range(1, Y):
            total = total + y2r[nth, d - 1].astype(jnp.float32)
        out[:, j * W : (j + 1) * W] = total[:, :W]
        out[:, R + j * W : R + (j + 1) * W] = total[:, W:]

    order = list(range(1, NB - 1)) + [0, NB - 1]
    for t in range(NB + 4):
        if t < NB:
            if order[t] == 0:
                fill_halo()
            level_one(order[t], t)
        if t == 0:
            turn_columns()
        if 0 <= t - 1 < NB:
            sum_y(t - 1)
        if t < NB:
            sum_cores(t)
        if 0 <= t - 1 < NB:
            level_two(order[t - 1], t - 1)
        if 0 <= t - 3 < NB:
            sum_x(t - 3)
        if 0 <= t - 4 < NB:
            finish(order[t - 4], t - 4)

    sent = [u2_copy]
    for group in (core_copy, y_copy, l_copy, x_copy, y2_copy):
        sent.extend(group.values())
    for copy in sent:
        copy.wait_send()

    @pl.when(z < Z - 1)
    def _():
        right.wait_send()

    @pl.when(z > 0)
    def _():
        left.wait_send()


def shards(echoes, exponents, replica, interp0, upsample1, phase1, upsample2, phase2):
    S, L, _, R = echoes.shape
    G = upsample2.shape[0]
    B0 = interp0.shape[3]
    B1 = upsample1.shape[3]
    B2 = upsample2.shape[3]
    C, F, Z = lax.axis_size("coarse"), lax.axis_size("fine"), lax.axis_size("swath")
    Y = F // 2
    K = S // G
    nb = B1 // F
    wedge = B2 // (C * F)
    W = CHUNK
    NB = R // W
    half = (replica.shape[1] - 1) // 2
    bf16, f32 = jnp.bfloat16, jnp.float32

    ph1 = phase1.transpose(1, 0, 2)
    ph2 = phase2.transpose(1, 0, 2).reshape(G, C * Y, 2, wedge, R)

    dims = (C, Y, Z, G, K, S, L, B0, nb, wedge, NB, half)
    dma = pltpu.SemaphoreType.DMA
    vm = pltpu.VMEM
    spec = pl.BlockSpec(memory_space=pltpu.VMEM)
    flat = pl.pallas_call(
        functools.partial(kernel, dims),
        out_shape=jax.ShapeDtypeStruct((wedge, 2 * R), f32),
        in_specs=[spec] * 6 + [pl.BlockSpec(memory_space=pl.ANY), spec],
        out_specs=spec,
        scratch_shapes=[
            vm((2, 3 * W), f32),
            vm(upsample2.shape, bf16),
            vm((S, B0, 2 * L), bf16),
            vm((S, B1, 2 * B0), bf16),
            vm((G, C * Y, 2, wedge, 2 * nb), bf16),
            vm((2, S * L, R + 2 * W), bf16),
            vm((2, S * L, W), bf16),
            vm((2, S * L, W), bf16),
            vm((2, 3 * W, 2 * W), bf16),
            vm((S, 2 * B0, 2 * W), bf16),
            vm((G, 4 * nb, 2 * W), bf16),
            vm((G, C * Y, wedge, 2 * nb), bf16),
            vm((NB, Y, G, nb, 2 * W), f32),
            vm((NB, Y, G, nb, 2 * W), bf16),
            vm((NB, Y, G, nb, 2 * W), bf16),
            vm((NB, Y - 1, G, nb, 2 * W), bf16),
            vm((NB, Y - 1, G, nb, 2 * W), bf16),
            vm((NB, G, nb, 2 * W), bf16),
            vm((NB, G, nb, 2 * W), bf16),
            vm((NB, C - 1, Y, wedge, 2 * W), bf16),
            vm((NB, C - 1, Y, wedge, 2 * W), bf16),
            vm((NB, Y, wedge, 2 * W), f32),
            vm((NB, Y - 1, wedge, 2 * W), bf16),
            vm((NB, Y - 1, wedge, 2 * W), bf16),
            dma((1,)),
            dma((2,)),
            dma((2, 2)),
            dma((NB, Y, 2)),
            dma((NB, Y - 1, 2)),
            dma((NB, 2)),
            dma((NB, C - 1, Y, 2)),
            dma((NB, Y - 1, 2)),
        ],
        compiler_params=pltpu.CompilerParams(
            collective_id=0, has_side_effects=True, vmem_limit_bytes=28 * 1024 * 1024
        ),
    )(echoes, exponents.transpose(0, 2, 1), replica, interp0, upsample1, ph1, upsample2, ph2)
    return flat.reshape(wedge, 2, R)


def solution(mesh):
    in_specs = (
        P(("coarse", "fine"), None, None, "swath"),
        P(("coarse", "fine"), None, "swath"),
        P(),
        P(None, ("coarse", "fine"), None, None),
        P(None, ("coarse", "fine"), None, None),
        P(None, ("coarse", "fine"), "swath"),
        P("coarse", None, "fine", None),
        P(None, "coarse", "swath"),
    )
    out_specs = P(("coarse", "fine"), None, "swath")
    return jax.shard_map(shards, mesh=mesh, in_specs=in_specs, out_specs=out_specs, check_vma=False)
```

```python
import functools

import jax
import jax.numpy as jnp
from jax import lax
from jax.experimental import pallas as pl
from jax.experimental.pallas import tpu as pltpu
from jax.sharding import PartitionSpec as P

MESH = pl.DeviceIdType.MESH
CHUNK = 128

SIN = (0.7071067690849304, -0.029462767764925957, 0.0003682722744997591, -2.1886112335778307e-06, 7.1958234926228215e-09)
COS = (1.4142135381698608, -0.17677636444568634, 0.0036825749557465315, -3.061256938963197e-05, 1.2790442838195304e-07)


def horner(coefs, u):
    total = coefs[-1] * u + coefs[-2]
    for coef in coefs[-3::-1]:
        total = total * u + coef
    return total


def cos_sin(angles):
    x = angles.astype(jnp.float32)
    u = x * x
    s = x * horner(SIN, u)
    c = horner(COS, u)
    return 1.0 - s * s, s * c


def mixed(values):
    re = values[:, :CHUNK]
    im = values[:, CHUNK:]
    return jnp.concatenate([values, jnp.concatenate([-im, re], axis=1)], axis=0)


def turned(values, angles):
    cosine, sine = cos_sin(angles)
    re = values[:, :CHUNK]
    im = values[:, CHUNK:]
    return cosine * re - sine * im, sine * re + cosine * im


def dot(a, b):
    return jnp.dot(a, b, preferred_element_type=jnp.float32)


def kernel(
    dims, echoes, exponents, replica, interp0, upsample1, ph1, u2_hbm, ph2, out,
    hp, u2, w0, w1, u2t, xs, halo_l, halo_r, band, rhs1, rhs2, u2m, pown, pms, pmr, ys, yr, lown, lmr, xsnd, xrcv, ysnd, yrcv, own_x, own_y, y2s, y2r, x2s, x2r,
    load_sem, u2_sem, halo_sem, core_sem, y_sem, l_sem, x_sem, yf_sem, y2_sem, x2_sem,
):
    C, Y, Z, G, K, S, L, B0, nb, wedge, NB, half = dims
    W = CHUNK
    R = NB * W
    c = lax.axis_index("coarse")
    f = lax.axis_index("fine")
    z = lax.axis_index("swath")
    y = f // 2
    k = f % 2
    mate = {"fine": y * 2 + 1 - k}

    def y_peer(d):
        return {"fine": ((y + d) % Y) * 2 + k}

    def x_peer(e):
        return {"coarse": (c + e) % C}

    load = pltpu.make_async_copy(u2_hbm, u2, load_sem.at[0])
    load.start()

    barrier = pltpu.get_barrier_semaphore()
    partners = [mate] + [y_peer(d) for d in range(1, Y)] + [x_peer(e) for e in range(1, C)]
    for who in partners:
        pl.semaphore_signal(barrier, inc=1, device_id=who, device_id_type=MESH)

    @pl.when(z < Z - 1)
    def _():
        pl.semaphore_signal(barrier, inc=1, device_id={"swath": z + 1}, device_id_type=MESH)

    @pl.when(z > 0)
    def _():
        pl.semaphore_signal(barrier, inc=1, device_id={"swath": z - 1}, device_id_type=MESH)

    blocks = exponents.shape[1]
    spread = lax.broadcasted_iota(jnp.int32, (blocks, R), 1) // (R // blocks)
    spread = (spread == lax.broadcasted_iota(jnp.int32, (blocks, R), 0)).astype(jnp.bfloat16)
    for s in range(S):
        powers = jnp.left_shift(jnp.ones_like(exponents[s]), exponents[s]).astype(jnp.float32) * 2.0**-8
        factors = dot(powers.T.astype(jnp.bfloat16), spread)
        for part in range(2):
            values = echoes[s, :, part, :].astype(jnp.float32) * factors
            xs[part, s * L : (s + 1) * L, W : W + R] = values.astype(jnp.bfloat16)

    ends = jnp.where(z > 0, 1, 0) + jnp.where(z < Z - 1, 1, 0)
    pl.semaphore_wait(barrier, len(partners) + ends)

    def remote(src, dst, sems, who):
        return pltpu.make_async_remote_copy(
            src_ref=src, dst_ref=dst, send_sem=sems.at[0], recv_sem=sems.at[1], device_id=who, device_id_type=MESH
        )

    right = remote(xs.at[:, :, pl.ds(R, W)], halo_l, halo_sem.at[0], {"swath": jnp.minimum(z + 1, Z - 1)})
    left = remote(xs.at[:, :, pl.ds(W, W)], halo_r, halo_sem.at[1], {"swath": jnp.maximum(z - 1, 0)})

    @pl.when(z < Z - 1)
    def _():
        right.start()

    @pl.when(z > 0)
    def _():
        left.start()

    for s in range(S):
        w0[s] = jnp.concatenate([interp0[0, s], interp0[1, s]], axis=0).T
        w1[s] = jnp.concatenate([upsample1[0, s], upsample1[1, s]], axis=0).T

    reach = 3 * W
    hp[...] = jnp.zeros_like(hp)
    hp[:, : replica.shape[1]] = replica[...].astype(jnp.float32)
    toeplitz = []
    for part in range(2):
        row = jnp.broadcast_to(hp[part : part + 1, :], (W, reach))
        rolled = pltpu.roll(row, W - half, 1, stride=1, stride_axis=0)
        toeplitz.append(rolled.T.astype(jnp.bfloat16))
    band[0, :, :W] = toeplitz[0]
    band[0, :, W:] = -toeplitz[1]
    band[1, :, :W] = toeplitz[1]
    band[1, :, W:] = toeplitz[0]

    def fill_halo():
        @pl.when(z > 0)
        def _():
            right.wait_recv()
            xs[:, :, 0:W] = halo_l[...]

        @pl.when(z == 0)
        def _():
            xs[:, :, 0:W] = jnp.zeros((2, S * L, W), jnp.bfloat16)

        @pl.when(z < Z - 1)
        def _():
            left.wait_recv()
            xs[:, :, W + R : R + 2 * W] = halo_r[...]

        @pl.when(z == Z - 1)
        def _():
            xs[:, :, W + R : R + 2 * W] = jnp.zeros((2, S * L, W), jnp.bfloat16)

    core_copy, y_copy, l_copy, x_copy, yf_copy, y2_copy, x2_copy = {}, {}, {}, {}, {}, {}, {}
    u2_copy = remote(u2t.at[:, :, 1 - k], u2m, u2_sem, mate)
    sub = 64
    hw = wedge // 2

    def turn_columns():
        load.wait()
        step = max(wedge, W)
        for g in range(G):
            for first in range(0, u2.shape[3], step):
                block = u2[g, :, :, first : first + step].reshape(2 * nb, step).T
                for i in range(step // wedge):
                    q = first // wedge + i
                    u2t[g, q // 2, q % 2] = block[i * wedge : (i + 1) * wedge]
        u2_copy.start()

    def level_one(j, nth):
        lanes = pl.ds(j * W, W)
        window = pl.ds(j * W, reach)
        comp = (dot(xs[0, :, window], band[0]) + dot(xs[1, :, window], band[1])).astype(jnp.bfloat16)
        for s in range(S):
            beams = dot(w0[s], mixed(comp[s * L : (s + 1) * L])).astype(jnp.bfloat16)
            rhs1[s] = mixed(beams)
        def block(core, d, store):
            base = pl.multiple_of((((y + d) % Y) * 2 + core) * nb, nb)
            for g in range(G):
                values = [dot(w1[g * K + kid, pl.ds(base, nb), :], rhs1[g * K + kid]) for kid in range(K)]
                for start in range(0, nb, sub):
                    size = min(sub, nb - start)
                    rows = pl.ds(pl.multiple_of(base + start, size), size)
                    re = im = 0.0
                    for kid in range(K):
                        r, i = turned(values[kid][start : start + size], ph1[g * K + kid, rows, lanes])
                        re = re + r
                        im = im + i
                    store[g, start : start + size, :W] = re.astype(store.dtype)
                    store[g, start : start + size, W:] = im.astype(store.dtype)

        offsets = list(range(1, Y)) + [0]
        for d in offsets:
            block(1 - k, d, pms.at[nth, d])
            copy = remote(pms.at[nth, d], pmr.at[nth, d], core_sem.at[nth, d], mate)
            copy.start()
            core_copy[nth, d] = copy
        for d in offsets:
            block(k, d, pown.at[nth, d])

    def sum_cores(nth):
        for d in range(1, Y):
            core_copy[nth, d].wait_recv()
            for g in range(G):
                ys[nth, d - 1, g] = (pown[nth, d, g] + pmr[nth, d, g].astype(jnp.float32)).astype(jnp.bfloat16)
            copy = remote(ys.at[nth, d - 1], yr.at[nth, d - 1], y_sem.at[nth, d - 1], y_peer(d))
            copy.start()
            y_copy[nth, d] = copy

    def sum_y(nth):
        core_copy[nth, 0].wait_recv()
        for d in range(1, Y):
            y_copy[nth, d].wait_recv()
        for g in range(G):
            total = pown[nth, 0, g] + pmr[nth, 0, g].astype(jnp.float32)
            for d in range(1, Y):
                total = total + yr[nth, d - 1, g].astype(jnp.float32)
            lown[nth, g] = total.astype(jnp.bfloat16)
        copy = remote(lown.at[nth], lmr.at[nth], l_sem.at[nth], mate)
        copy.start()
        l_copy[nth] = copy

    def level_two(j, nth):
        if nth == 0:
            u2_copy.wait_recv()
        l_copy[nth].wait_recv()
        lanes = pl.ds(j * W, W)
        for g in range(G):
            rhs2[g, : 2 * nb] = mixed(lown[nth, g])
            rhs2[g, 2 * nb :] = mixed(lmr[nth, g])

        def block(e, d, stores):
            q = ((c + e) % C) * Y + (y + d) % Y
            values = [dot(jnp.concatenate([u2t[g, q, k], u2m[g, q]], axis=1), rhs2[g]) for g in range(G)]
            for h, store in enumerate(stores):
                for at in range(0, hw, sub):
                    size = min(sub, hw - at)
                    start = h * hw + at
                    re = im = 0.0
                    for g in range(G):
                        r, i = turned(values[g][start : start + size], ph2[g, q, k, start : start + size, lanes])
                        re = re + r
                        im = im + i
                    store[at : at + size, :W] = re.astype(store.dtype)
                    store[at : at + size, W:] = im.astype(store.dtype)

        for e in list(range(1, C)) + [0]:
            for d in list(range(1, Y)) + [0]:
                first = xsnd.at[nth, e - 1, d] if e else own_x.at[nth, d]
                second = ysnd.at[nth, d - 1, e] if d else own_y.at[nth, e]
                block(e, d, (first, second))
                if e:
                    at = (nth, e - 1, d)
                    x_copy[nth, e, d] = remote(xsnd.at[at], xrcv.at[at], x_sem.at[at], x_peer(e))
                    x_copy[nth, e, d].start()
                if d:
                    at = (nth, d - 1, e)
                    yf_copy[nth, d, e] = remote(ysnd.at[at], yrcv.at[at], yf_sem.at[at], y_peer(d))
                    yf_copy[nth, d, e].start()

    def summed_x(nth, d):
        total = own_x[nth, d]
        for e in range(1, C):
            x_copy[nth, e, d].wait_recv()
            total = total + xrcv[nth, e - 1, d].astype(jnp.float32)
        return total

    def summed_y(nth, e):
        total = own_y[nth, e]
        for d in range(1, Y):
            yf_copy[nth, d, e].wait_recv()
            total = total + yrcv[nth, d - 1, e].astype(jnp.float32)
        return total

    def second_hop(nth):
        for d in range(1, Y):
            at = (nth, d - 1)
            y2s[at] = summed_x(nth, d).astype(jnp.bfloat16)
            y2_copy[nth, d] = remote(y2s.at[at], y2r.at[at], y2_sem.at[at], y_peer(d))
            y2_copy[nth, d].start()
        for e in range(1, C):
            at = (nth, e - 1)
            x2s[at] = summed_y(nth, e).astype(jnp.bfloat16)
            x2_copy[nth, e] = remote(x2s.at[at], x2r.at[at], x2_sem.at[at], x_peer(e))
            x2_copy[nth, e].start()

    def finish(j, nth):
        lanes = pl.ds(j * W, W)
        total = summed_x(nth, 0)
        for d in range(1, Y):
            y2_copy[nth, d].wait_recv()
            total = total + y2r[nth, d - 1].astype(jnp.float32)
        out[0, :hw, lanes] = total[:, :W]
        out[1, :hw, lanes] = total[:, W:]
        total = summed_y(nth, 0)
        for e in range(1, C):
            x2_copy[nth, e].wait_recv()
            total = total + x2r[nth, e - 1].astype(jnp.float32)
        out[0, hw:, lanes] = total[:, :W]
        out[1, hw:, lanes] = total[:, W:]

    order = list(range(1, NB - 1)) + [0, NB - 1]
    for t in range(NB + 4):
        if t < NB:
            if order[t] == 0:
                fill_halo()
            level_one(order[t], t)
        if t == 0:
            turn_columns()
        if 0 <= t - 1 < NB:
            sum_y(t - 1)
        if t < NB:
            sum_cores(t)
        if 0 <= t - 1 < NB:
            level_two(order[t - 1], t - 1)
        if 0 <= t - 3 < NB:
            second_hop(t - 3)
        if 0 <= t - 4 < NB:
            finish(order[t - 4], t - 4)

    sent = [u2_copy]
    for group in (core_copy, y_copy, l_copy, x_copy, yf_copy, y2_copy, x2_copy):
        sent.extend(group.values())
    for copy in sent:
        copy.wait_send()

    @pl.when(z < Z - 1)
    def _():
        right.wait_send()

    @pl.when(z > 0)
    def _():
        left.wait_send()


def shards(echoes, exponents, replica, interp0, upsample1, phase1, upsample2, phase2):
    S, L, _, R = echoes.shape
    G = upsample2.shape[0]
    B0 = interp0.shape[3]
    B1 = upsample1.shape[3]
    B2 = upsample2.shape[3]
    C, F, Z = lax.axis_size("coarse"), lax.axis_size("fine"), lax.axis_size("swath")
    Y = F // 2
    K = S // G
    nb = B1 // F
    wedge = B2 // (C * F)
    W = CHUNK
    NB = R // W
    hw = wedge // 2
    half = (replica.shape[1] - 1) // 2
    bf16, f32 = jnp.bfloat16, jnp.float32

    ph1 = phase1.transpose(1, 0, 2)
    ph2 = phase2.transpose(1, 0, 2).reshape(G, C * Y, 2, wedge, R)

    dims = (C, Y, Z, G, K, S, L, B0, nb, wedge, NB, half)
    dma = pltpu.SemaphoreType.DMA
    vm = pltpu.VMEM
    spec = pl.BlockSpec(memory_space=pltpu.VMEM)
    planes = pl.pallas_call(
        functools.partial(kernel, dims),
        out_shape=jax.ShapeDtypeStruct((2, wedge, R), f32),
        in_specs=[spec] * 6 + [pl.BlockSpec(memory_space=pl.ANY), spec],
        out_specs=spec,
        scratch_shapes=[
            vm((2, 3 * W), f32),
            vm(upsample2.shape, bf16),
            vm((S, B0, 2 * L), bf16),
            vm((S, B1, 2 * B0), bf16),
            vm((G, C * Y, 2, wedge, 2 * nb), bf16),
            vm((2, S * L, R + 2 * W), bf16),
            vm((2, S * L, W), bf16),
            vm((2, S * L, W), bf16),
            vm((2, 3 * W, 2 * W), bf16),
            vm((S, 2 * B0, 2 * W), bf16),
            vm((G, 4 * nb, 2 * W), bf16),
            vm((G, C * Y, wedge, 2 * nb), bf16),
            vm((NB, Y, G, nb, 2 * W), f32),
            vm((NB, Y, G, nb, 2 * W), bf16),
            vm((NB, Y, G, nb, 2 * W), bf16),
            vm((NB, Y - 1, G, nb, 2 * W), bf16),
            vm((NB, Y - 1, G, nb, 2 * W), bf16),
            vm((NB, G, nb, 2 * W), bf16),
            vm((NB, G, nb, 2 * W), bf16),
            vm((NB, C - 1, Y, hw, 2 * W), bf16),
            vm((NB, C - 1, Y, hw, 2 * W), bf16),
            vm((NB, Y - 1, C, hw, 2 * W), bf16),
            vm((NB, Y - 1, C, hw, 2 * W), bf16),
            vm((NB, Y, hw, 2 * W), f32),
            vm((NB, C, hw, 2 * W), f32),
            vm((NB, Y - 1, hw, 2 * W), bf16),
            vm((NB, Y - 1, hw, 2 * W), bf16),
            vm((NB, C - 1, hw, 2 * W), bf16),
            vm((NB, C - 1, hw, 2 * W), bf16),
            dma((1,)),
            dma((2,)),
            dma((2, 2)),
            dma((NB, Y, 2)),
            dma((NB, Y - 1, 2)),
            dma((NB, 2)),
            dma((NB, C - 1, Y, 2)),
            dma((NB, Y - 1, C, 2)),
            dma((NB, Y - 1, 2)),
            dma((NB, C - 1, 2)),
        ],
        compiler_params=pltpu.CompilerParams(
            collective_id=0, has_side_effects=True, vmem_limit_bytes=28 * 1024 * 1024
        ),
    )(echoes, exponents.transpose(0, 2, 1), replica, interp0, upsample1, ph1, upsample2, ph2)
    return planes.transpose(1, 0, 2)


def solution(mesh):
    in_specs = (
        P(("coarse", "fine"), None, None, "swath"),
        P(("coarse", "fine"), None, "swath"),
        P(),
        P(None, ("coarse", "fine"), None, None),
        P(None, ("coarse", "fine"), None, None),
        P(None, ("coarse", "fine"), "swath"),
        P("coarse", None, "fine", None),
        P(None, "coarse", "swath"),
    )
    out_specs = P(("coarse", "fine"), None, "swath")
    return jax.shard_map(shards, mesh=mesh, in_specs=in_specs, out_specs=out_specs, check_vma=False)
```

```python
import functools

import jax
import jax.numpy as jnp
from jax import lax
from jax.experimental import pallas as pl
from jax.experimental.pallas import tpu as pltpu
from jax.sharding import PartitionSpec as P

MESH = pl.DeviceIdType.MESH
CHUNK = 128

SIN = (0.7071067690849304, -0.029462767764925957, 0.0003682722744997591, -2.1886112335778307e-06, 7.1958234926228215e-09)
COS = (1.4142135381698608, -0.17677636444568634, 0.0036825749557465315, -3.061256938963197e-05, 1.2790442838195304e-07)


def horner(coefs, u):
    total = coefs[-1] * u + coefs[-2]
    for coef in coefs[-3::-1]:
        total = total * u + coef
    return total


def cos_sin(angles):
    x = angles.astype(jnp.float32)
    u = x * x
    s = x * horner(SIN, u)
    c = horner(COS, u)
    return 1.0 - s * s, s * c


def mixed(values):
    re = values[:, :CHUNK]
    im = values[:, CHUNK:]
    return jnp.concatenate([values, jnp.concatenate([-im, re], axis=1)], axis=0)


def turned(values, angles):
    cosine, sine = cos_sin(angles)
    re = values[:, :CHUNK]
    im = values[:, CHUNK:]
    return cosine * re - sine * im, sine * re + cosine * im


def dot(a, b):
    return jnp.dot(a, b, preferred_element_type=jnp.float32)


def kernel(
    dims, echoes, exponents, replica, interp0, upsample1, ph1, u2_hbm, ph2, out,
    hp, u2, w0, w1, u2t, xs, halo_l, halo_r, band, rhs1, rhs2, u2m, pown, pms, pmr, ys, yr, lown, lmr, snd, xrcv, yrcv, own, y2s, y2r, x2s, x2r,
    load_sem, u2_sem, halo_sem, core_sem, y_sem, l_sem, x_sem, yf_sem, y2_sem, x2_sem,
):
    C, Y, Z, G, K, S, L, B0, nb, wedge, NB, half = dims
    W = CHUNK
    R = NB * W
    c = lax.axis_index("coarse")
    f = lax.axis_index("fine")
    z = lax.axis_index("swath")
    y = f // 2
    k = f % 2
    mate = {"fine": y * 2 + 1 - k}

    def y_peer(d):
        return {"fine": ((y + d) % Y) * 2 + k}

    def x_peer(e):
        return {"coarse": (c + e) % C}

    load = pltpu.make_async_copy(u2_hbm, u2, load_sem.at[0])
    load.start()

    barrier = pltpu.get_barrier_semaphore()
    partners = [mate] + [y_peer(d) for d in range(1, Y)] + [x_peer(e) for e in range(1, C)]
    for who in partners:
        pl.semaphore_signal(barrier, inc=1, device_id=who, device_id_type=MESH)

    @pl.when(z < Z - 1)
    def _():
        pl.semaphore_signal(barrier, inc=1, device_id={"swath": z + 1}, device_id_type=MESH)

    @pl.when(z > 0)
    def _():
        pl.semaphore_signal(barrier, inc=1, device_id={"swath": z - 1}, device_id_type=MESH)

    blocks = exponents.shape[1]
    spread = lax.broadcasted_iota(jnp.int32, (blocks, R), 1) // (R // blocks)
    spread = (spread == lax.broadcasted_iota(jnp.int32, (blocks, R), 0)).astype(jnp.bfloat16)
    for s in range(S):
        powers = jnp.left_shift(jnp.ones_like(exponents[s]), exponents[s]).astype(jnp.float32) * 2.0**-8
        factors = dot(powers.T.astype(jnp.bfloat16), spread)
        for part in range(2):
            values = echoes[s, :, part, :].astype(jnp.float32) * factors
            xs[part, s * L : (s + 1) * L, W : W + R] = values.astype(jnp.bfloat16)

    ends = jnp.where(z > 0, 1, 0) + jnp.where(z < Z - 1, 1, 0)
    pl.semaphore_wait(barrier, len(partners) + ends)

    def remote(src, dst, sems, who):
        return pltpu.make_async_remote_copy(
            src_ref=src, dst_ref=dst, send_sem=sems.at[0], recv_sem=sems.at[1], device_id=who, device_id_type=MESH
        )

    right = remote(xs.at[:, :, pl.ds(R, W)], halo_l, halo_sem.at[0], {"swath": jnp.minimum(z + 1, Z - 1)})
    left = remote(xs.at[:, :, pl.ds(W, W)], halo_r, halo_sem.at[1], {"swath": jnp.maximum(z - 1, 0)})

    @pl.when(z < Z - 1)
    def _():
        right.start()

    @pl.when(z > 0)
    def _():
        left.start()

    for s in range(S):
        w0[s] = jnp.concatenate([interp0[0, s], interp0[1, s]], axis=0).T
        w1[s] = jnp.concatenate([upsample1[0, s], upsample1[1, s]], axis=0).T

    reach = 3 * W
    hp[...] = jnp.zeros_like(hp)
    hp[:, : replica.shape[1]] = replica[...].astype(jnp.float32)
    toeplitz = []
    for part in range(2):
        row = jnp.broadcast_to(hp[part : part + 1, :], (W, reach))
        rolled = pltpu.roll(row, W - half, 1, stride=1, stride_axis=0)
        toeplitz.append(rolled.T.astype(jnp.bfloat16))
    band[0, :, :W] = toeplitz[0]
    band[0, :, W:] = -toeplitz[1]
    band[1, :, :W] = toeplitz[1]
    band[1, :, W:] = toeplitz[0]

    def fill_halo():
        @pl.when(z > 0)
        def _():
            right.wait_recv()
            xs[:, :, 0:W] = halo_l[...]

        @pl.when(z == 0)
        def _():
            xs[:, :, 0:W] = jnp.zeros((2, S * L, W), jnp.bfloat16)

        @pl.when(z < Z - 1)
        def _():
            left.wait_recv()
            xs[:, :, W + R : R + 2 * W] = halo_r[...]

        @pl.when(z == Z - 1)
        def _():
            xs[:, :, W + R : R + 2 * W] = jnp.zeros((2, S * L, W), jnp.bfloat16)

    core_copy, y_copy, l_copy, x_copy, yf_copy, y2_copy, x2_copy = {}, {}, {}, {}, {}, {}, {}
    u2_copy = remote(u2t.at[:, :, 1 - k], u2m, u2_sem, mate)
    sub = 64
    hw = wedge // 2

    def turn_columns():
        load.wait()
        step = max(wedge, W)
        steps = u2.shape[3] // step

        @pl.loop(0, G * steps)
        def _(t):
            g = t // steps
            first = pl.multiple_of((t % steps) * step, step)
            block = u2[g, :, :, pl.ds(first, step)].reshape(2 * nb, step).T
            for i in range(step // wedge):
                q = (t % steps) * (step // wedge) + i
                u2t[g, q // 2, q % 2] = block[i * wedge : (i + 1) * wedge]

        u2_copy.start()

    def level_one(j, nth):
        lanes = pl.ds(j * W, W)
        window = pl.ds(j * W, reach)
        comp = (dot(xs[0, :, window], band[0]) + dot(xs[1, :, window], band[1])).astype(jnp.bfloat16)
        for s in range(S):
            beams = dot(w0[s], mixed(comp[s * L : (s + 1) * L])).astype(jnp.bfloat16)
            rhs1[s] = mixed(beams)
        def blocks(core, store):
            @pl.loop(0, Y * G)
            def _(t):
                d = t // G
                g = t % G
                base = pl.multiple_of((((y + d) % Y) * 2 + core) * nb, nb)
                values = [dot(w1[g * K + kid, pl.ds(base, nb), :], rhs1[g * K + kid]) for kid in range(K)]
                for start in range(0, nb, sub):
                    size = min(sub, nb - start)
                    rows = pl.ds(pl.multiple_of(base + start, size), size)
                    re = im = 0.0
                    for kid in range(K):
                        r, i = turned(values[kid][start : start + size], ph1[g * K + kid, rows, lanes])
                        re = re + r
                        im = im + i
                    store[d, g, start : start + size, :W] = re.astype(store.dtype)
                    store[d, g, start : start + size, W:] = im.astype(store.dtype)

        blocks(1 - k, pms.at[nth])
        for d in range(Y):
            copy = remote(pms.at[nth, d], pmr.at[nth, d], core_sem.at[nth, d], mate)
            copy.start()
            core_copy[nth, d] = copy
        blocks(k, pown.at[nth])

    def sum_cores(nth):
        for d in range(1, Y):
            core_copy[nth, d].wait_recv()
            for g in range(G):
                ys[nth, d - 1, g] = (pown[nth, d, g] + pmr[nth, d, g].astype(jnp.float32)).astype(jnp.bfloat16)
            copy = remote(ys.at[nth, d - 1], yr.at[nth, d - 1], y_sem.at[nth, d - 1], y_peer(d))
            copy.start()
            y_copy[nth, d] = copy

    def sum_y(nth):
        core_copy[nth, 0].wait_recv()
        for d in range(1, Y):
            y_copy[nth, d].wait_recv()
        for g in range(G):
            total = pown[nth, 0, g] + pmr[nth, 0, g].astype(jnp.float32)
            for d in range(1, Y):
                total = total + yr[nth, d - 1, g].astype(jnp.float32)
            lown[nth, g] = total.astype(jnp.bfloat16)
        copy = remote(lown.at[nth], lmr.at[nth], l_sem.at[nth], mate)
        copy.start()
        l_copy[nth] = copy

    def level_two(j, nth):
        if nth == 0:
            u2_copy.wait_recv()
        l_copy[nth].wait_recv()
        lanes = pl.ds(j * W, W)
        for g in range(G):
            rhs2[g, : 2 * nb] = mixed(lown[nth, g])
            rhs2[g, 2 * nb :] = mixed(lmr[nth, g])

        @pl.loop(0, C * Y)
        def _(t):
            e = t // Y
            d = t % Y
            q = ((c + e) % C) * Y + (y + d) % Y
            values = [dot(jnp.concatenate([u2t[g, q, k], u2m[g, q]], axis=1), rhs2[g]) for g in range(G)]
            for h in range(2):
                for at in range(0, hw, sub):
                    size = min(sub, hw - at)
                    start = h * hw + at
                    re = im = 0.0
                    for g in range(G):
                        r, i = turned(values[g][start : start + size], ph2[g, q, k, start : start + size, lanes])
                        re = re + r
                        im = im + i
                    own[nth, h, e, d, at : at + size, :W] = re
                    own[nth, h, e, d, at : at + size, W:] = im
                    snd[nth, h, e, d, at : at + size, :W] = re.astype(jnp.bfloat16)
                    snd[nth, h, e, d, at : at + size, W:] = im.astype(jnp.bfloat16)

        for e in list(range(1, C)) + [0]:
            for d in list(range(1, Y)) + [0]:
                if e:
                    at = (nth, e - 1, d)
                    x_copy[nth, e, d] = remote(snd.at[nth, 0, e, d], xrcv.at[at], x_sem.at[at], x_peer(e))
                    x_copy[nth, e, d].start()
                if d:
                    at = (nth, d - 1, e)
                    yf_copy[nth, d, e] = remote(snd.at[nth, 1, e, d], yrcv.at[at], yf_sem.at[at], y_peer(d))
                    yf_copy[nth, d, e].start()

    def summed_x(nth, d):
        total = own[nth, 0, 0, d]
        for e in range(1, C):
            x_copy[nth, e, d].wait_recv()
            total = total + xrcv[nth, e - 1, d].astype(jnp.float32)
        return total

    def summed_y(nth, e):
        total = own[nth, 1, e, 0]
        for d in range(1, Y):
            yf_copy[nth, d, e].wait_recv()
            total = total + yrcv[nth, d - 1, e].astype(jnp.float32)
        return total

    def second_hop(nth):
        for d in range(1, Y):
            at = (nth, d - 1)
            y2s[at] = summed_x(nth, d).astype(jnp.bfloat16)
            y2_copy[nth, d] = remote(y2s.at[at], y2r.at[at], y2_sem.at[at], y_peer(d))
            y2_copy[nth, d].start()
        for e in range(1, C):
            at = (nth, e - 1)
            x2s[at] = summed_y(nth, e).astype(jnp.bfloat16)
            x2_copy[nth, e] = remote(x2s.at[at], x2r.at[at], x2_sem.at[at], x_peer(e))
            x2_copy[nth, e].start()

    def finish(j, nth):
        lanes = pl.ds(j * W, W)
        total = summed_x(nth, 0)
        for d in range(1, Y):
            y2_copy[nth, d].wait_recv()
            total = total + y2r[nth, d - 1].astype(jnp.float32)
        out[0, :hw, lanes] = total[:, :W]
        out[1, :hw, lanes] = total[:, W:]
        total = summed_y(nth, 0)
        for e in range(1, C):
            x2_copy[nth, e].wait_recv()
            total = total + x2r[nth, e - 1].astype(jnp.float32)
        out[0, hw:, lanes] = total[:, :W]
        out[1, hw:, lanes] = total[:, W:]

    order = list(range(1, NB - 1)) + [0, NB - 1]
    for t in range(NB + 4):
        if t < NB:
            if order[t] == 0:
                fill_halo()
            level_one(order[t], t)
        if 0 <= t - 1 < NB:
            sum_y(t - 1)
        if t < NB:
            sum_cores(t)
        if t == 0:
            turn_columns()
        if 0 <= t - 1 < NB:
            level_two(order[t - 1], t - 1)
        if 0 <= t - 3 < NB:
            second_hop(t - 3)
        if 0 <= t - 4 < NB:
            finish(order[t - 4], t - 4)

    sent = [u2_copy]
    for group in (core_copy, y_copy, l_copy, x_copy, yf_copy, y2_copy, x2_copy):
        sent.extend(group.values())
    for copy in sent:
        copy.wait_send()

    @pl.when(z < Z - 1)
    def _():
        right.wait_send()

    @pl.when(z > 0)
    def _():
        left.wait_send()


def shards(echoes, exponents, replica, interp0, upsample1, phase1, upsample2, phase2):
    S, L, _, R = echoes.shape
    G = upsample2.shape[0]
    B0 = interp0.shape[3]
    B1 = upsample1.shape[3]
    B2 = upsample2.shape[3]
    C, F, Z = lax.axis_size("coarse"), lax.axis_size("fine"), lax.axis_size("swath")
    Y = F // 2
    K = S // G
    nb = B1 // F
    wedge = B2 // (C * F)
    W = CHUNK
    NB = R // W
    hw = wedge // 2
    half = (replica.shape[1] - 1) // 2
    bf16, f32 = jnp.bfloat16, jnp.float32

    ph1 = phase1.transpose(1, 0, 2)
    ph2 = phase2.transpose(1, 0, 2).reshape(G, C * Y, 2, wedge, R)

    dims = (C, Y, Z, G, K, S, L, B0, nb, wedge, NB, half)
    dma = pltpu.SemaphoreType.DMA
    vm = pltpu.VMEM
    spec = pl.BlockSpec(memory_space=pltpu.VMEM)
    planes = pl.pallas_call(
        functools.partial(kernel, dims),
        out_shape=jax.ShapeDtypeStruct((2, wedge, R), f32),
        in_specs=[spec] * 6 + [pl.BlockSpec(memory_space=pl.ANY), spec],
        out_specs=spec,
        scratch_shapes=[
            vm((2, 3 * W), f32),
            vm(upsample2.shape, bf16),
            vm((S, B0, 2 * L), bf16),
            vm((S, B1, 2 * B0), bf16),
            vm((G, C * Y, 2, wedge, 2 * nb), bf16),
            vm((2, S * L, R + 2 * W), bf16),
            vm((2, S * L, W), bf16),
            vm((2, S * L, W), bf16),
            vm((2, 3 * W, 2 * W), bf16),
            vm((S, 2 * B0, 2 * W), bf16),
            vm((G, 4 * nb, 2 * W), bf16),
            vm((G, C * Y, wedge, 2 * nb), bf16),
            vm((NB, Y, G, nb, 2 * W), f32),
            vm((NB, Y, G, nb, 2 * W), bf16),
            vm((NB, Y, G, nb, 2 * W), bf16),
            vm((NB, Y - 1, G, nb, 2 * W), bf16),
            vm((NB, Y - 1, G, nb, 2 * W), bf16),
            vm((NB, G, nb, 2 * W), bf16),
            vm((NB, G, nb, 2 * W), bf16),
            vm((NB, 2, C, Y, hw, 2 * W), bf16),
            vm((NB, C - 1, Y, hw, 2 * W), bf16),
            vm((NB, Y - 1, C, hw, 2 * W), bf16),
            vm((NB, 2, C, Y, hw, 2 * W), f32),
            vm((NB, Y - 1, hw, 2 * W), bf16),
            vm((NB, Y - 1, hw, 2 * W), bf16),
            vm((NB, C - 1, hw, 2 * W), bf16),
            vm((NB, C - 1, hw, 2 * W), bf16),
            dma((1,)),
            dma((2,)),
            dma((2, 2)),
            dma((NB, Y, 2)),
            dma((NB, Y - 1, 2)),
            dma((NB, 2)),
            dma((NB, C - 1, Y, 2)),
            dma((NB, Y - 1, C, 2)),
            dma((NB, Y - 1, 2)),
            dma((NB, C - 1, 2)),
        ],
        compiler_params=pltpu.CompilerParams(
            collective_id=0, has_side_effects=True, vmem_limit_bytes=32 * 1024 * 1024
        ),
    )(echoes, exponents.transpose(0, 2, 1), replica, interp0, upsample1, ph1, upsample2, ph2)
    return planes.transpose(1, 0, 2)


def solution(mesh):
    in_specs = (
        P(("coarse", "fine"), None, None, "swath"),
        P(("coarse", "fine"), None, "swath"),
        P(),
        P(None, ("coarse", "fine"), None, None),
        P(None, ("coarse", "fine"), None, None),
        P(None, ("coarse", "fine"), "swath"),
        P("coarse", None, "fine", None),
        P(None, "coarse", "swath"),
    )
    out_specs = P(("coarse", "fine"), None, "swath")
    return jax.shard_map(shards, mesh=mesh, in_specs=in_specs, out_specs=out_specs, check_vma=False)
```

```python
import functools

import jax
import jax.numpy as jnp
from jax import lax
from jax.experimental import pallas as pl
from jax.experimental.pallas import tpu as pltpu
from jax.sharding import PartitionSpec as P

MESH = pl.DeviceIdType.MESH
CHUNK = 128

SIN = (0.7071067690849304, -0.029462767764925957, 0.0003682722744997591, -2.1886112335778307e-06, 7.1958234926228215e-09)
COS = (1.4142135381698608, -0.17677636444568634, 0.0036825749557465315, -3.061256938963197e-05, 1.2790442838195304e-07)


def horner(coefs, u):
    total = coefs[-1] * u + coefs[-2]
    for coef in coefs[-3::-1]:
        total = total * u + coef
    return total


def cos_sin(angles):
    x = angles.astype(jnp.float32)
    u = x * x
    s = x * horner(SIN, u)
    c = horner(COS, u)
    return 1.0 - s * s, s * c


def mixed(values):
    re = values[:, :CHUNK]
    im = values[:, CHUNK:]
    return jnp.concatenate([values, jnp.concatenate([-im, re], axis=1)], axis=0)


def turned(values, angles):
    cosine, sine = cos_sin(angles)
    re = values[:, :CHUNK]
    im = values[:, CHUNK:]
    return cosine * re - sine * im, sine * re + cosine * im


def dot(a, b):
    return jnp.dot(a, b, preferred_element_type=jnp.float32)


def kernel(
    dims, echoes, exponents, replica, interp0, upsample1, ph1, u2_hbm, ph2, out,
    hp, u2, w0, w1, u2t, xs, halo_l, halo_r, band, rhs1, rhs2, u2m, pown, pms, pmr, ys, yr, lown, lmr, xsnd, xrcv, ysnd, yrcv, own_x, own_y, y2s, y2r, x2s, x2r,
    load_sem, u2_sem, halo_sem, core_sem, y_sem, l_sem, x_sem, yf_sem, y2_sem, x2_sem,
):
    C, Y, Z, G, K, S, L, B0, nb, wedge, NB, half = dims
    W = CHUNK
    R = NB * W
    c = lax.axis_index("coarse")
    f = lax.axis_index("fine")
    z = lax.axis_index("swath")
    y = f // 2
    k = f % 2
    mate = {"fine": y * 2 + 1 - k}

    def y_peer(d):
        return {"fine": ((y + d) % Y) * 2 + k}

    def x_peer(e):
        return {"coarse": (c + e) % C}

    load = pltpu.make_async_copy(u2_hbm, u2, load_sem.at[0])
    load.start()

    barrier = pltpu.get_barrier_semaphore()
    partners = [mate] + [y_peer(d) for d in range(1, Y)] + [x_peer(e) for e in range(1, C)]
    for who in partners:
        pl.semaphore_signal(barrier, inc=1, device_id=who, device_id_type=MESH)

    @pl.when(z < Z - 1)
    def _():
        pl.semaphore_signal(barrier, inc=1, device_id={"swath": z + 1}, device_id_type=MESH)

    @pl.when(z > 0)
    def _():
        pl.semaphore_signal(barrier, inc=1, device_id={"swath": z - 1}, device_id_type=MESH)

    blocks = exponents.shape[1]
    spread = lax.broadcasted_iota(jnp.int32, (blocks, R), 1) // (R // blocks)
    spread = (spread == lax.broadcasted_iota(jnp.int32, (blocks, R), 0)).astype(jnp.bfloat16)
    for s in range(S):
        powers = jnp.left_shift(jnp.ones_like(exponents[s]), exponents[s]).astype(jnp.float32) * 2.0**-8
        factors = dot(powers.T.astype(jnp.bfloat16), spread)
        for part in range(2):
            values = echoes[s, :, part, :].astype(jnp.float32) * factors
            xs[part, s * L : (s + 1) * L, W : W + R] = values.astype(jnp.bfloat16)

    ends = jnp.where(z > 0, 1, 0) + jnp.where(z < Z - 1, 1, 0)
    pl.semaphore_wait(barrier, len(partners) + ends)

    def remote(src, dst, sems, who):
        return pltpu.make_async_remote_copy(
            src_ref=src, dst_ref=dst, send_sem=sems.at[0], recv_sem=sems.at[1], device_id=who, device_id_type=MESH
        )

    right = remote(xs.at[:, :, pl.ds(R, W)], halo_l, halo_sem.at[0], {"swath": jnp.minimum(z + 1, Z - 1)})
    left = remote(xs.at[:, :, pl.ds(W, W)], halo_r, halo_sem.at[1], {"swath": jnp.maximum(z - 1, 0)})

    @pl.when(z < Z - 1)
    def _():
        right.start()

    @pl.when(z > 0)
    def _():
        left.start()

    for s in range(S):
        w0[s] = jnp.concatenate([interp0[0, s], interp0[1, s]], axis=0).T
        w1[s] = jnp.concatenate([upsample1[0, s], upsample1[1, s]], axis=0).T

    reach = 3 * W
    hp[...] = jnp.zeros_like(hp)
    hp[:, : replica.shape[1]] = replica[...].astype(jnp.float32)
    toeplitz = []
    for part in range(2):
        row = jnp.broadcast_to(hp[part : part + 1, :], (W, reach))
        rolled = pltpu.roll(row, W - half, 1, stride=1, stride_axis=0)
        toeplitz.append(rolled.T.astype(jnp.bfloat16))
    band[0, :, :W] = toeplitz[0]
    band[0, :, W:] = -toeplitz[1]
    band[1, :, :W] = toeplitz[1]
    band[1, :, W:] = toeplitz[0]

    def fill_halo():
        @pl.when(z > 0)
        def _():
            right.wait_recv()
            xs[:, :, 0:W] = halo_l[...]

        @pl.when(z == 0)
        def _():
            xs[:, :, 0:W] = jnp.zeros((2, S * L, W), jnp.bfloat16)

        @pl.when(z < Z - 1)
        def _():
            left.wait_recv()
            xs[:, :, W + R : R + 2 * W] = halo_r[...]

        @pl.when(z == Z - 1)
        def _():
            xs[:, :, W + R : R + 2 * W] = jnp.zeros((2, S * L, W), jnp.bfloat16)

    core_copy, y_copy, l_copy, x_copy, yf_copy, y2_copy, x2_copy = {}, {}, {}, {}, {}, {}, {}
    u2_copy = remote(u2t.at[:, :, 1 - k], u2m, u2_sem, mate)
    sub = 32
    hw = wedge // 2

    def turn_columns():
        load.wait()
        step = max(wedge, W)
        for g in range(G):
            for first in range(0, u2.shape[3], step):
                block = u2[g, :, :, first : first + step].reshape(2 * nb, step).T
                for i in range(step // wedge):
                    q = first // wedge + i
                    u2t[g, q // 2, q % 2] = block[i * wedge : (i + 1) * wedge]
        u2_copy.start()

    def level_one(j, nth):
        lanes = pl.ds(j * W, W)
        window = pl.ds(j * W, reach)
        comp = (dot(xs[0, :, window], band[0]) + dot(xs[1, :, window], band[1])).astype(jnp.bfloat16)
        for s in range(S):
            beams = dot(w0[s], mixed(comp[s * L : (s + 1) * L])).astype(jnp.bfloat16)
            rhs1[s] = mixed(beams)
        def block(core, d, store):
            base = pl.multiple_of((((y + d) % Y) * 2 + core) * nb, nb)
            for g in range(G):
                values = [dot(w1[g * K + kid, pl.ds(base, nb), :], rhs1[g * K + kid]) for kid in range(K)]
                for start in range(0, nb, sub):
                    size = min(sub, nb - start)
                    rows = pl.ds(pl.multiple_of(base + start, size), size)
                    re = im = 0.0
                    for kid in range(K):
                        r, i = turned(values[kid][start : start + size], ph1[g * K + kid, rows, lanes])
                        re = re + r
                        im = im + i
                    store[g, start : start + size, :W] = re.astype(store.dtype)
                    store[g, start : start + size, W:] = im.astype(store.dtype)

        offsets = list(range(1, Y)) + [0]
        for d in offsets:
            block(1 - k, d, pms.at[nth, d])
            copy = remote(pms.at[nth, d], pmr.at[nth, d], core_sem.at[nth, d], mate)
            copy.start()
            core_copy[nth, d] = copy
        for d in offsets:
            block(k, d, pown.at[nth, d])

    def sum_cores(nth):
        for d in range(1, Y):
            core_copy[nth, d].wait_recv()
            for g in range(G):
                ys[nth, d - 1, g] = (pown[nth, d, g] + pmr[nth, d, g].astype(jnp.float32)).astype(jnp.bfloat16)
            copy = remote(ys.at[nth, d - 1], yr.at[nth, d - 1], y_sem.at[nth, d - 1], y_peer(d))
            copy.start()
            y_copy[nth, d] = copy

    def sum_y(nth):
        core_copy[nth, 0].wait_recv()
        for d in range(1, Y):
            y_copy[nth, d].wait_recv()
        for g in range(G):
            total = pown[nth, 0, g] + pmr[nth, 0, g].astype(jnp.float32)
            for d in range(1, Y):
                total = total + yr[nth, d - 1, g].astype(jnp.float32)
            lown[nth, g] = total.astype(jnp.bfloat16)
        copy = remote(lown.at[nth], lmr.at[nth], l_sem.at[nth], mate)
        copy.start()
        l_copy[nth] = copy

    def level_two(j, nth):
        if nth == 0:
            u2_copy.wait_recv()
        l_copy[nth].wait_recv()
        lanes = pl.ds(j * W, W)
        for g in range(G):
            rhs2[g, : 2 * nb] = mixed(lown[nth, g])
            rhs2[g, 2 * nb :] = mixed(lmr[nth, g])

        def block(e, d, stores):
            q = ((c + e) % C) * Y + (y + d) % Y
            values = [dot(jnp.concatenate([u2t[g, q, k], u2m[g, q]], axis=1), rhs2[g]) for g in range(G)]
            for h, store in enumerate(stores):
                for at in range(0, hw, sub):
                    size = min(sub, hw - at)
                    start = h * hw + at
                    re = im = 0.0
                    for g in range(G):
                        r, i = turned(values[g][start : start + size], ph2[g, q, k, start : start + size, lanes])
                        re = re + r
                        im = im + i
                    store[at : at + size, :W] = re.astype(store.dtype)
                    store[at : at + size, W:] = im.astype(store.dtype)

        for e in list(range(1, C)) + [0]:
            for d in list(range(1, Y)) + [0]:
                first = xsnd.at[nth, e - 1, d] if e else own_x.at[nth, d]
                second = ysnd.at[nth, d - 1, e] if d else own_y.at[nth, e]
                block(e, d, (first, second))
                if e:
                    at = (nth, e - 1, d)
                    x_copy[nth, e, d] = remote(xsnd.at[at], xrcv.at[at], x_sem.at[at], x_peer(e))
                    x_copy[nth, e, d].start()
                if d:
                    at = (nth, d - 1, e)
                    yf_copy[nth, d, e] = remote(ysnd.at[at], yrcv.at[at], yf_sem.at[at], y_peer(d))
                    yf_copy[nth, d, e].start()

    def summed_x(nth, d):
        total = own_x[nth, d]
        for e in range(1, C):
            x_copy[nth, e, d].wait_recv()
            total = total + xrcv[nth, e - 1, d].astype(jnp.float32)
        return total

    def summed_y(nth, e):
        total = own_y[nth, e]
        for d in range(1, Y):
            yf_copy[nth, d, e].wait_recv()
            total = total + yrcv[nth, d - 1, e].astype(jnp.float32)
        return total

    def second_hop(nth):
        for d in range(1, Y):
            at = (nth, d - 1)
            y2s[at] = summed_x(nth, d).astype(jnp.bfloat16)
            y2_copy[nth, d] = remote(y2s.at[at], y2r.at[at], y2_sem.at[at], y_peer(d))
            y2_copy[nth, d].start()
        for e in range(1, C):
            at = (nth, e - 1)
            x2s[at] = summed_y(nth, e).astype(jnp.bfloat16)
            x2_copy[nth, e] = remote(x2s.at[at], x2r.at[at], x2_sem.at[at], x_peer(e))
            x2_copy[nth, e].start()

    def finish(j, nth):
        lanes = pl.ds(j * W, W)
        total = summed_x(nth, 0)
        for d in range(1, Y):
            y2_copy[nth, d].wait_recv()
            total = total + y2r[nth, d - 1].astype(jnp.float32)
        out[0, :hw, lanes] = total[:, :W]
        out[1, :hw, lanes] = total[:, W:]
        total = summed_y(nth, 0)
        for e in range(1, C):
            x2_copy[nth, e].wait_recv()
            total = total + x2r[nth, e - 1].astype(jnp.float32)
        out[0, hw:, lanes] = total[:, :W]
        out[1, hw:, lanes] = total[:, W:]

    order = list(range(1, NB - 1)) + [0, NB - 1]
    for t in range(NB + 4):
        if t < NB:
            if order[t] == 0:
                fill_halo()
            level_one(order[t], t)
        if 0 <= t - 1 < NB:
            sum_y(t - 1)
        if t < NB:
            sum_cores(t)
        if t == 0:
            turn_columns()
        if 0 <= t - 1 < NB:
            level_two(order[t - 1], t - 1)
        if 0 <= t - 3 < NB:
            second_hop(t - 3)
        if 0 <= t - 4 < NB:
            finish(order[t - 4], t - 4)

    sent = [u2_copy]
    for group in (core_copy, y_copy, l_copy, x_copy, yf_copy, y2_copy, x2_copy):
        sent.extend(group.values())
    for copy in sent:
        copy.wait_send()

    @pl.when(z < Z - 1)
    def _():
        right.wait_send()

    @pl.when(z > 0)
    def _():
        left.wait_send()


def shards(echoes, exponents, replica, interp0, upsample1, phase1, upsample2, phase2):
    S, L, _, R = echoes.shape
    G = upsample2.shape[0]
    B0 = interp0.shape[3]
    B1 = upsample1.shape[3]
    B2 = upsample2.shape[3]
    C, F, Z = lax.axis_size("coarse"), lax.axis_size("fine"), lax.axis_size("swath")
    Y = F // 2
    K = S // G
    nb = B1 // F
    wedge = B2 // (C * F)
    W = CHUNK
    NB = R // W
    hw = wedge // 2
    half = (replica.shape[1] - 1) // 2
    bf16, f32 = jnp.bfloat16, jnp.float32

    ph1 = phase1.transpose(1, 0, 2)
    ph2 = phase2.transpose(1, 0, 2).reshape(G, C * Y, 2, wedge, R)

    dims = (C, Y, Z, G, K, S, L, B0, nb, wedge, NB, half)
    dma = pltpu.SemaphoreType.DMA
    vm = pltpu.VMEM
    spec = pl.BlockSpec(memory_space=pltpu.VMEM)
    planes = pl.pallas_call(
        functools.partial(kernel, dims),
        out_shape=jax.ShapeDtypeStruct((2, wedge, R), f32),
        in_specs=[spec] * 6 + [pl.BlockSpec(memory_space=pl.ANY), spec],
        out_specs=spec,
        scratch_shapes=[
            vm((2, 3 * W), f32),
            vm(upsample2.shape, bf16),
            vm((S, B0, 2 * L), bf16),
            vm((S, B1, 2 * B0), bf16),
            vm((G, C * Y, 2, wedge, 2 * nb), bf16),
            vm((2, S * L, R + 2 * W), bf16),
            vm((2, S * L, W), bf16),
            vm((2, S * L, W), bf16),
            vm((2, 3 * W, 2 * W), bf16),
            vm((S, 2 * B0, 2 * W), bf16),
            vm((G, 4 * nb, 2 * W), bf16),
            vm((G, C * Y, wedge, 2 * nb), bf16),
            vm((NB, Y, G, nb, 2 * W), f32),
            vm((NB, Y, G, nb, 2 * W), bf16),
            vm((NB, Y, G, nb, 2 * W), bf16),
            vm((NB, Y - 1, G, nb, 2 * W), bf16),
            vm((NB, Y - 1, G, nb, 2 * W), bf16),
            vm((NB, G, nb, 2 * W), bf16),
            vm((NB, G, nb, 2 * W), bf16),
            vm((NB, C - 1, Y, hw, 2 * W), bf16),
            vm((NB, C - 1, Y, hw, 2 * W), bf16),
            vm((NB, Y - 1, C, hw, 2 * W), bf16),
            vm((NB, Y - 1, C, hw, 2 * W), bf16),
            vm((NB, Y, hw, 2 * W), f32),
            vm((NB, C, hw, 2 * W), f32),
            vm((NB, Y - 1, hw, 2 * W), bf16),
            vm((NB, Y - 1, hw, 2 * W), bf16),
            vm((NB, C - 1, hw, 2 * W), bf16),
            vm((NB, C - 1, hw, 2 * W), bf16),
            dma((1,)),
            dma((2,)),
            dma((2, 2)),
            dma((NB, Y, 2)),
            dma((NB, Y - 1, 2)),
            dma((NB, 2)),
            dma((NB, C - 1, Y, 2)),
            dma((NB, Y - 1, C, 2)),
            dma((NB, Y - 1, 2)),
            dma((NB, C - 1, 2)),
        ],
        compiler_params=pltpu.CompilerParams(
            collective_id=0, has_side_effects=True, vmem_limit_bytes=28 * 1024 * 1024
        ),
    )(echoes, exponents.transpose(0, 2, 1), replica, interp0, upsample1, ph1, upsample2, ph2)
    return planes.transpose(1, 0, 2)


def solution(mesh):
    in_specs = (
        P(("coarse", "fine"), None, None, "swath"),
        P(("coarse", "fine"), None, "swath"),
        P(),
        P(None, ("coarse", "fine"), None, None),
        P(None, ("coarse", "fine"), None, None),
        P(None, ("coarse", "fine"), "swath"),
        P("coarse", None, "fine", None),
        P(None, "coarse", "swath"),
    )
    out_specs = P(("coarse", "fine"), None, "swath")
    return jax.shard_map(shards, mesh=mesh, in_specs=in_specs, out_specs=out_specs, check_vma=False)
```
